32 devices in a mesh: dp: 8 (over z, core), expert: 4 (over y, x).
Axes of the slice: x: 2, y: 2, z: 4, core: 2. Of those that a mesh axis runs over, the one named last changes fastest.
Arguments:
- tokens: bfloat16 [4096, 2048], P(('dp', 'expert')), may hold values from -6 to 6
- queries: bfloat16 [4096, 128], P(('dp', 'expert')), may hold values from -4.5 to 4.5
- key_vectors: bfloat16 [4096, 128], P(('dp', 'expert')), may hold values from -4.5 to 4.5
- gate_logits: float32 [4096, 8], P(('dp', 'expert')), may hold values from -6 to 6
- value_routes: int32 [4096, 2], P(('dp', 'expert')), may hold values from 0 to 3, all different within a row; in each aligned block of 128 rows (0 to 127, 128 to 255, ...) at most 80 rows name the same one
- output_routes: int32 [4096, 2], P(('dp', 'expert')), may hold values from 0 to 3, all different within a row; in each aligned block of 128 rows (0 to 127, 128 to 255, ...) at most 80 rows name the same one
- value_weight: bfloat16 [4, 2048, 128], P('expert', 'dp'), may hold values from -0.125 to 0.125
- output_weight: bfloat16 [4, 2048, 128], P('expert', 'dp'), may hold values from -0.5 to 0.5
- cotangent: bfloat16 [4096, 2048], P(('dp', 'expert')), may hold values from -6 to 6
Outputs:
- token_grad: bfloat16 [4096, 2048], P(('dp', 'expert'))
- query_grad: bfloat16 [4096, 128], P(('dp', 'expert'))
- key_grad: bfloat16 [4096, 128], P(('dp', 'expert'))
- logit_grad: float32 [4096, 8], P(('dp', 'expert'))
- value_weight_grad: float32 [4, 2048, 128], P('expert', 'dp')
- output_weight_grad: float32 [4, 2048, 128], P('expert', 'dp')
The draws below stay inside these ranges and needn't reach their ends.
Inputs may be any that keep to these rules, and one draw needn't show every extreme that they name: `value_routes`: among one device's 128 tokens no value expert is named more than 80 times, a bound that some block reaches. `output_routes`: among one device's 128 tokens no output expert is named more than 80 times, a bound that some block reaches.
All inputs are finite; a program needn't handle non-finite values.
Results may differ from the reference program's by a relative error of at most 0.025.
Values may be sent and summed in bfloat16 or wider, within the bound.
No kernel may reach another device: no remote copies, remote signals or barrier semaphores. Data moves between devices by JAX's collectives and lax.ppermute only.
A program may use at most 64 MiB of HBM per device.

```python
import math
import jax
import jax.numpy as jnp
import numpy as np
from jax import lax

D = 2048
HD = 128
TOK_DEV = 128
E = 4
CAP = 80
TOKENS = 4096
N_DP = 8


def attention_pair(key):
    base_query = jnp.clip(jax.random.normal(jax.random.fold_in(key, 101), (TOKENS, HD), jnp.float32), -4.5, 4.5)
    base_key = jnp.clip(jax.random.normal(jax.random.fold_in(key, 102), (TOKENS, HD), jnp.float32), -4.5, 4.5)
    return (base_query, base_key)


def draw_queries(key, part):
    return attention_pair(key)[0].astype(jnp.bfloat16)


def draw_key_vectors(key, part):
    return attention_pair(key)[1].astype(jnp.bfloat16)


def spiked(values, own_key, source, target, shards_of, factor):
    owner, partner = [(jnp.arange(values.shape[position]) // (values.shape[position] // shards_of)).reshape([-1 if axis == position else 1 for axis in range(values.ndim)]) for position in (source, target)]
    chosen = jax.random.permutation(own_key, shards_of)[partner]
    strong = (owner == chosen) | (owner == (partner + shards_of // 2) % shards_of)
    return jnp.where(strong, factor * values, values)


def levels(key, extent, pieces, least, largest):
    level = 1.0
    for dim, shards_of in pieces:
        heights = jax.random.uniform(jax.random.fold_in(jax.random.fold_in(key, 6), dim), (shards_of,), jnp.float32, least / len(pieces), largest / len(pieces))
        level = level * jnp.repeat(jnp.exp(heights), extent[dim] // shards_of).reshape((-1,) + (1,) * (len(extent) - 1 - dim))
    return level


def assign_block(key, own, number, rows, number_of, top, bound, lean):
    ranking = jax.random.permutation(key, number_of)
    heavy_load, common = load_shares(number_of, rows * top, bound, lean, True), load_shares(number_of, rows * top, bound, lean, False)
    places = jnp.arange(number_of)

    def named(sizes, rotation):
        used = int((sizes > 0).sum())
        fixed = max(1, used // 4)
        shifted = fixed + (places - fixed + rotation * (used - fixed)) % max(1, number_of - fixed)
        return jnp.zeros((number_of,), jnp.int32).at[ranking[jnp.where(places < fixed, places, shifted)]].set(jnp.asarray(sizes, jnp.int32))

    sizes = jnp.where(number % 4 == 0, named(heavy_load, number // 4), named(common, number - number // 4 - 1))
    mixed = jax.random.permutation(jax.random.fold_in(own, 3), number_of)
    source_of, sink = mixed[0:number_of // 2 * 2:2], mixed[1:number_of // 2 * 2:2]
    slack = jnp.minimum(sizes[source_of] - 1, bound - sizes[sink]) // 2
    slack = jnp.where((source_of == ranking[0]) | (sink == ranking[0]) | (sizes[sink] == 0), 0, jnp.maximum(slack, 0))
    shifted = jax.random.randint(jax.random.fold_in(own, 4), (number_of // 2,), 0, 1 << 20) % (slack + 1)
    sizes = sizes.at[source_of].add(-shifted).at[sink].add(shifted)
    labels = jnp.searchsorted(jnp.cumsum(sizes), jnp.arange(rows * top), side="right").astype(jnp.int32)
    grid = labels.reshape(top, rows).T
    grid = grid[jax.random.permutation(jax.random.fold_in(own, 1), rows)]
    rotation = jax.random.randint(jax.random.fold_in(own, 2), (rows, 1), 0, top)
    return jnp.take_along_axis(grid, (jnp.arange(top)[None, :] + rotation) % top, axis=1)


def load_shares(number_of, total, reach, slope, full):
    loads = [(1 << 20) // math.isqrt(standing ** slope) + 1 for standing in range(1, number_of + 1)]
    largest = reach if full else min(reach, max(-(-total // number_of), total * loads[0] // sum(loads)))
    least = 1 if total - largest >= number_of - 1 else 0
    counts, rest = [largest] + [least] * (number_of - 1), total - largest - least * (number_of - 1)
    while rest > 0:
        candidates = [i for i in range(1, number_of) if counts[i] < largest] or [i for i in range(1, number_of) if counts[i] < reach]
        pool, left = sum([loads[i] for i in candidates]), rest
        for i in candidates:
            extra = min(reach - counts[i], max(1, left * loads[i] // pool), rest)
            counts[i] = counts[i] + extra
            rest = rest - extra
    return np.array(counts)


def gaussian(own_key, extent, deviation, limit, cuts=(), kind=jnp.bfloat16):
    values = deviation * jax.random.normal(own_key, extent, jnp.float32)
    if cuts:
        values = values * levels(own_key, extent, cuts, -0.22, 0.18)
    return jnp.clip(values, -limit, limit).astype(kind)


def noise_with(rng, shape, width, limit, shards, heavy, held_as=jnp.bfloat16):
    result = width * jax.random.normal(rng, shape, jnp.float32)
    if shards:
        result = result * levels(rng, shape, shards, -0.22, 0.18)
    return jnp.clip(spiked(result, jax.random.fold_in(rng, 3), *heavy), -limit, limit).astype(held_as)


def setup_inputs(seed: int = 0) -> dict:
    keys = jax.random.split(jax.random.key(seed), 10)
    tokens = noise_with(keys[0], (TOKENS, D), 1.0, 6.0, ((0, 32),), (0, 1, 32, 2.75))
    queries = draw_queries(jax.random.fold_in(keys[9], 71), 0)
    key_vectors = draw_key_vectors(jax.random.fold_in(keys[9], 71), 0)
    gate_logits = gaussian(keys[3], (TOKENS, 2 * E), 1.5, 6.0, ((0, 32),), jnp.float32)
    value_routes_keys = jax.random.split(jax.random.fold_in(keys[4], 1), TOKENS // TOK_DEV)
    value_routes_turns = jax.random.permutation(jax.random.fold_in(keys[4], 3), TOKENS // TOK_DEV)
    value_routes = jax.vmap(lambda own, number: assign_block(jax.random.fold_in(keys[4], 2), own, number, TOK_DEV, E, 2, CAP, 2))(value_routes_keys, value_routes_turns).reshape((TOKENS, 2))
    output_routes_keys = jax.random.split(jax.random.fold_in(keys[5], 1), TOKENS // TOK_DEV)
    output_routes_turns = jax.random.permutation(jax.random.fold_in(keys[5], 3), TOKENS // TOK_DEV)
    output_routes = jax.vmap(lambda own, number: assign_block(jax.random.fold_in(keys[5], 2), own, number, TOK_DEV, E, 2, CAP, 2))(output_routes_keys, output_routes_turns).reshape((TOKENS, 2))
    value_weight = gaussian(keys[6], (E, D, HD), D ** -0.5, 0.125, ((0, 4), (1, 8)))
    output_weight = gaussian(keys[7], (E, D, HD), HD ** -0.5, 0.5, ((0, 4), (1, 8)))
    cotangent = noise_with(keys[8], (TOKENS, D), 1.0, 6.0, ((0, 32),), (0, 1, 32, 2.75))
    return {"tokens": tokens, "queries": queries, "key_vectors": key_vectors, "gate_logits": gate_logits, "value_routes": value_routes, "output_routes": output_routes, "value_weight": value_weight, "output_weight": output_weight, "cotangent": cotangent}


def slot_index(routes, experts, capacity):
    flattened = routes.reshape(-1)
    onehot = (flattened[:, None] == jnp.arange(experts, dtype=jnp.int32)[None, :]).astype(jnp.int32)
    before = jnp.cumsum(onehot, axis=0) - onehot
    return (flattened * capacity + lax.optimization_barrier(jnp.sum(before * onehot, axis=1))).astype(jnp.int32)

def owner_rows(slots, experts, capacity):
    row_count = slots.shape[0]
    owner_table = jnp.full((experts * capacity,), row_count, jnp.int32)
    return owner_table.at[slots].set(jnp.arange(row_count, dtype=jnp.int32))

def causal_probs(queries, key_vectors):
    length_rows = queries.shape[0]
    scores = jnp.dot(queries, key_vectors.T, preferred_element_type=jnp.float32) / math.sqrt(queries.shape[1])
    row_ids = lax.broadcasted_iota(jnp.int32, (length_rows, length_rows), 0)
    col_ids = lax.broadcasted_iota(jnp.int32, (length_rows, length_rows), 1)
    scores = jnp.where(row_ids >= col_ids, scores, -1e+30)
    row_max = lax.optimization_barrier(jnp.max(scores, axis=1, keepdims=True))
    exponent = jnp.exp(scores - row_max)
    return exponent / lax.optimization_barrier(jnp.sum(exponent, axis=1, keepdims=True))

def attend(packed):
    probs = causal_probs(packed[0], packed[1])
    weights = probs.astype(jnp.bfloat16)
    return jnp.dot(weights, packed[2], preferred_element_type=jnp.float32).astype(jnp.bfloat16)

def attend_back(packed):
    queries, key_vectors, mixed_value, hidden_grad = packed
    probs = causal_probs(queries, key_vectors)
    weights = probs.astype(jnp.bfloat16)
    prob_grad = jnp.dot(hidden_grad, mixed_value.T, preferred_element_type=jnp.float32)
    score_grad = probs * (prob_grad - lax.optimization_barrier(jnp.sum(prob_grad * probs, axis=1, keepdims=True)))
    scaled_grad = (score_grad / math.sqrt(queries.shape[1])).astype(jnp.bfloat16)
    query_grad = jnp.dot(scaled_grad, key_vectors, preferred_element_type=jnp.float32).astype(jnp.bfloat16)
    key_grad = jnp.dot(scaled_grad.T, queries, preferred_element_type=jnp.float32).astype(jnp.bfloat16)
    value_grad = jnp.dot(weights.T, hidden_grad, preferred_element_type=jnp.float32).astype(jnp.bfloat16)
    return (query_grad, key_grad, value_grad)

def group_sum(row_block, other_rows):
    partials = jnp.einsum('gnd,gnh->gdh', row_block.reshape(N_DP, -1, D).astype(jnp.float32), other_rows.reshape(N_DP, -1, HD).astype(jnp.float32))
    rounded = lax.optimization_barrier(partials.astype(jnp.bfloat16))
    return lax.optimization_barrier(jnp.sum(rounded.astype(jnp.float32), axis=0)) / N_DP

def reference(tokens, queries, key_vectors, gate_logits, value_routes, output_routes, value_weight, output_weight, cotangent):
    capacity = 5 * TOK_DEV // (2 * E)
    blocks = TOKENS // TOK_DEV
    pair_count = 2 * TOK_DEV
    gate_values = jax.nn.sigmoid(gate_logits)
    value_gate = jnp.take_along_axis(gate_values[:, :E], value_routes, axis=1)
    output_gate = jnp.take_along_axis(gate_values[:, E:], output_routes, axis=1)

    def block_slots(routes):
        return slot_index(routes, E, capacity)

    def block_owners(slots):
        return owner_rows(slots, E, capacity)
    slot_value = jax.vmap(block_slots)(value_routes.reshape(blocks, TOK_DEV, 2))
    slot_output = jax.vmap(block_slots)(output_routes.reshape(blocks, TOK_DEV, 2))

    def expert_index(owners):
        block_start = jnp.arange(blocks, dtype=jnp.int32)[:, None]
        token_index = jnp.where(owners < pair_count, block_start * TOK_DEV + owners // 2, TOKENS).astype(jnp.int32)
        pair_index = jnp.where(owners < pair_count, block_start * pair_count + owners, 2 * TOKENS).astype(jnp.int32)
        token_index = token_index.reshape(blocks, E, capacity).transpose(1, 0, 2).reshape(E, blocks * capacity)
        pair_index = pair_index.reshape(blocks, E, capacity).transpose(1, 0, 2).reshape(E, blocks * capacity)
        return (token_index, pair_index)
    token_value, pair_value = expert_index(jax.vmap(block_owners)(slot_value))
    token_output, pair_output = expert_index(jax.vmap(block_owners)(slot_output))

    def per_slot(results, slots):
        row_width = results.shape[-1]
        slot_grid = results.reshape(E, blocks, capacity, row_width).transpose(1, 0, 2, 3).reshape(blocks, E * capacity, row_width)

        def pick_rows(grid_block, slot_block):
            return grid_block[slot_block]
        return jax.vmap(pick_rows)(slot_grid, slots).reshape(TOKENS, 2, row_width)

    def value_expert(packed):
        row_block = jnp.take(tokens, packed[0], axis=0, mode='fill', fill_value=0)
        return jnp.dot(row_block, packed[1], preferred_element_type=jnp.float32).astype(jnp.bfloat16)
    expert_value = per_slot(lax.map(value_expert, (token_value, value_weight)), slot_value).astype(jnp.float32)
    mixed_value = lax.optimization_barrier(jnp.sum(value_gate[:, :, None] * expert_value, axis=1)).astype(jnp.bfloat16)

    def by_sequence(array):
        return array.reshape(blocks, TOK_DEV, array.shape[-1])
    hidden = lax.map(attend, (by_sequence(queries), by_sequence(key_vectors), by_sequence(mixed_value))).reshape(TOKENS, HD)
    gated_hidden = (output_gate[:, :, None] * hidden[:, None, :].astype(jnp.float32)).astype(jnp.bfloat16).reshape(2 * TOKENS, HD)

    def output_expert(packed):
        row_block = jnp.take(cotangent, packed[0], axis=0, mode='fill', fill_value=0)
        gated_rows = jnp.take(gated_hidden, packed[1], axis=0, mode='fill', fill_value=0)
        returned = jnp.dot(row_block, packed[2], preferred_element_type=jnp.float32).astype(jnp.bfloat16)
        return (returned, group_sum(row_block, gated_rows))
    head_rows, output_weight_grad = lax.map(output_expert, (token_output, pair_output, output_weight))
    head_back = per_slot(head_rows, slot_output).astype(jnp.float32)
    output_gate_grad = lax.optimization_barrier(jnp.sum(hidden[:, None, :].astype(jnp.float32) * head_back, axis=2))
    hidden_grad = lax.optimization_barrier(jnp.sum(output_gate[:, :, None] * head_back, axis=1)).astype(jnp.bfloat16)
    query_grad, key_grad, value_grad = lax.map(attend_back, (by_sequence(queries), by_sequence(key_vectors), by_sequence(mixed_value), by_sequence(hidden_grad)))
    query_grad = query_grad.reshape(TOKENS, HD)
    key_grad = key_grad.reshape(TOKENS, HD)
    value_grad = value_grad.reshape(TOKENS, HD)
    gated_value = (value_gate[:, :, None] * value_grad[:, None, :].astype(jnp.float32)).astype(jnp.bfloat16).reshape(2 * TOKENS, HD)
    value_gate_grad = lax.optimization_barrier(jnp.sum(value_grad[:, None, :].astype(jnp.float32) * expert_value, axis=2))

    def value_backward(running, packed):
        row_block = jnp.take(tokens, packed[0], axis=0, mode='fill', fill_value=0)
        gated_rows = jnp.take(gated_value, packed[1], axis=0, mode='fill', fill_value=0)
        returned = lax.dot_general(gated_rows, packed[2], (((1,), (1,)), ((), ())), preferred_element_type=jnp.float32).astype(jnp.bfloat16)
        running = running.at[packed[0]].add(returned.astype(jnp.float32), mode='drop')
        return (running, group_sum(row_block, gated_rows))
    summed, value_weight_grad = lax.scan(value_backward, jnp.zeros((TOKENS, D), jnp.float32), (token_value, pair_value, value_weight))
    token_grad = summed.astype(jnp.bfloat16)
    expert_ids = jnp.arange(E, dtype=jnp.int32)[None, None, :]
    hot_value = (value_routes[:, :, None] == expert_ids).astype(jnp.float32)
    hot_output = (output_routes[:, :, None] == expert_ids).astype(jnp.float32)
    logit_value = lax.optimization_barrier(jnp.sum(hot_value * (value_gate_grad * value_gate * (1.0 - value_gate))[:, :, None], axis=1))
    logit_output = lax.optimization_barrier(jnp.sum(hot_output * (output_gate_grad * output_gate * (1.0 - output_gate))[:, :, None], axis=1))
    logit_grad = jnp.concatenate([logit_value, logit_output], axis=1)
    return (token_grad, query_grad, key_grad, logit_grad, value_weight_grad, output_weight_grad)
```

```python
import math

import jax
import jax.numpy as jnp
from jax import lax
from jax.experimental import pallas as pl
from jax.experimental.pallas import tpu as pltpu
from jax.sharding import PartitionSpec as P

F32, BF16 = jnp.float32, jnp.bfloat16
VALUE_GATE, OUTPUT_GATE, VALUE_ROUTE, OUTPUT_ROUTE, LOW_PART = 0, 2, 4, 6, 8


def kernel_call(body, outs, *args, scalars=0, flops=0):
    moved = sum(x.size * x.dtype.itemsize for x in args) + sum(
        math.prod(s) * jnp.dtype(t).itemsize for s, t in outs
    )
    return pl.pallas_call(
        body,
        out_shape=[jax.ShapeDtypeStruct(s, t) for s, t in outs],
        in_specs=[pl.BlockSpec(memory_space=pltpu.SMEM)] * scalars
        + [pl.BlockSpec(memory_space=pltpu.VMEM)] * (len(args) - scalars),
        out_specs=[pl.BlockSpec(memory_space=pltpu.VMEM)] * len(outs),
        cost_estimate=pl.CostEstimate(flops=flops, bytes_accessed=moved, transcendentals=0),
        compiler_params=pltpu.CompilerParams(vmem_limit_bytes=24 * 2**20),
    )(*args)


def dot(left, right):
    return jnp.dot(left, right, preferred_element_type=F32)


def dot_nt(left, right):
    return lax.dot_general(left, right, (((1,), (1,)), ((), ())), preferred_element_type=F32)


def table_body(me_ref, logits_ref, vr_ref, or_ref, q_ref, k_ref, table_ref, sent_ref, probs_ref, weights_ref, back_ref):
    rows, both = logits_ref.shape
    experts = both // 2
    gates = jax.nn.sigmoid(logits_ref[...])
    ids = lax.broadcasted_iota(jnp.int32, (rows, both), 1)
    lane = lax.broadcasted_iota(jnp.int32, table_ref.shape, 1)
    table = jnp.zeros(table_ref.shape, F32)
    for j in range(2):
        route_v, route_o = vr_ref[:, j : j + 1], or_ref[:, j : j + 1]
        gate_v = jnp.sum(jnp.where(ids == route_v, gates, 0.0), axis=1, keepdims=True)
        gate_o = jnp.sum(jnp.where(ids == route_o + experts, gates, 0.0), axis=1, keepdims=True)
        table = jnp.where(lane == VALUE_GATE + j, gate_v, table)
        table = jnp.where(lane == OUTPUT_GATE + j, gate_o, table)
        table = jnp.where(lane == VALUE_ROUTE + j, (route_v ^ me_ref[0]).astype(F32), table)
        table = jnp.where(lane == OUTPUT_ROUTE + j, (route_o ^ me_ref[0]).astype(F32), table)
    table_ref[...] = table
    high = table.astype(BF16).astype(F32)
    low = table - high
    for j in range(4):
        high = jnp.where(lane == LOW_PART + j, low[:, j : j + 1], high)
    sent_ref[...] = high.astype(BF16)
    length = q_ref.shape[0]
    scores = dot_nt(q_ref[...], k_ref[...]) / math.sqrt(q_ref.shape[1])
    row_ids = lax.broadcasted_iota(jnp.int32, (length, length), 0)
    col_ids = lax.broadcasted_iota(jnp.int32, (length, length), 1)
    scores = jnp.where(row_ids >= col_ids, scores, -1e30)
    exponent = jnp.exp(scores - jnp.max(scores, axis=1, keepdims=True))
    probs = exponent / jnp.sum(exponent, axis=1, keepdims=True)
    probs_ref[...] = probs
    weights_ref[...] = probs.astype(BF16)
    back_ref[...] = probs.T.astype(BF16)


def transpose_body(own_ref, got_ref, out_ref):
    rows, width = own_ref.shape
    out_ref[:, :rows] = own_ref[...].T
    out_ref[:, rows:] = got_ref[:, :width].T


def gate_columns(own_table, got_table, gate, route):
    columns = []
    for j in range(2):
        far_gate = got_table[:, gate + j : gate + j + 1].astype(F32) + got_table[
            :, LOW_PART + gate + j : LOW_PART + gate + j + 1
        ].astype(F32)
        columns.append(
            (
                jnp.concatenate([own_table[:, gate + j : gate + j + 1], far_gate], axis=0),
                jnp.concatenate(
                    [
                        own_table[:, route + j : route + j + 1],
                        got_table[:, route + j : route + j + 1].astype(F32),
                    ],
                    axis=0,
                ),
            )
        )
    return columns


def pair_up(refs):
    return [
        jnp.concatenate([r[...] for r in refs[i : i + 2]], axis=1) for i in range(0, len(refs), 2)
    ]


def partial_body(experts, gate, route, own_ref, got_ref, table_ref, got_table_ref, *refs):
    near, far, keep_ref, send_ref = refs[:experts], refs[experts : 2 * experts], refs[-2], refs[-1]
    rows, width = own_ref.shape
    half = width // 2
    left = jnp.concatenate([own_ref[...], got_ref[:, :width]], axis=0)
    columns = gate_columns(table_ref[...], got_table_ref[...], gate, route)
    slots = [jnp.zeros((2 * rows, near[0].shape[1]), F32) for _ in range(2)]
    size = near[0].shape[1]
    for i, (w_near, w_far) in enumerate(zip(pair_up(near), pair_up(far))):
        product = dot(left[:, :half], w_near) + dot(left[:, half:], w_far)
        for p in range(product.shape[1] // size):
            piece = product[:, p * size : (p + 1) * size]
            for j in range(2):
                slots[j] = jnp.where(columns[j][1] == float(2 * i + p), piece, slots[j])
    for j in range(2):
        keep_ref[:, j * size : (j + 1) * size] = slots[j][:rows]
        send_ref[:, j * size : (j + 1) * size] = slots[j][rows:].astype(BF16)


def hidden_body(keep_ref, got_ref, table_ref, weights_ref, value_ref, mixed_ref, hidden_ref):
    size = mixed_ref.shape[1]
    value = (keep_ref[...] + got_ref[...].astype(F32)).astype(BF16)
    value_ref[...] = value
    mixed = jnp.zeros(mixed_ref.shape, F32)
    for j in range(2):
        gate = table_ref[:, VALUE_GATE + j : VALUE_GATE + j + 1]
        mixed += gate * value[:, j * size : (j + 1) * size].astype(F32)
    mixed_ref[...] = mixed.astype(BF16)
    hidden_ref[...] = dot(weights_ref[...], mixed.astype(BF16)).astype(BF16)


def head_body(keep_ref, got_ref, table_ref, back_ref, head_ref, grad_ref, value_grad_ref):
    size = grad_ref.shape[1]
    head = (keep_ref[...] + got_ref[...].astype(F32)).astype(BF16)
    head_ref[...] = head
    grad = jnp.zeros(grad_ref.shape, F32)
    for j in range(2):
        gate = table_ref[:, OUTPUT_GATE + j : OUTPUT_GATE + j + 1]
        grad += gate * head[:, j * size : (j + 1) * size].astype(F32)
    grad_ref[...] = grad.astype(BF16)
    value_grad_ref[...] = dot(back_ref[...], grad.astype(BF16)).astype(BF16)


def gated_rows(experts, columns, rows):
    gated = []
    for k in range(experts):
        gate = sum(jnp.where(route == float(k), g, 0.0) for g, route in columns)
        gated.append((gate * rows).astype(BF16))
    return gated


def weight_grad_body(experts, gate, route, turned_ref, own_ref, got_ref, table_ref, got_table_ref, keep_ref, send_ref):
    rows = jnp.concatenate([own_ref[...], got_ref[...]], axis=0).astype(F32)
    columns = gate_columns(table_ref[...], got_table_ref[...], gate, route)
    gated = gated_rows(experts, columns, rows)
    half, size = turned_ref.shape[0] // 2, own_ref.shape[1]
    for i in range(0, experts, 2):
        right = jnp.concatenate(gated[i : i + 2], axis=1)
        product = dot(turned_ref[...], right)
        for p in range(right.shape[1] // size):
            piece = product[:, p * size : (p + 1) * size]
            keep_ref[i + p] = piece[:half]
            send_ref[i + p] = piece[half:].astype(BF16)


def core_sum_body(keep_ref, got_ref, own_ref, *send_refs):
    own_ref[...] = keep_ref[0] + got_ref[0].astype(F32)
    for k, send_ref in enumerate(send_refs):
        send_ref[...] = (keep_ref[k + 1] + got_ref[k + 1].astype(F32)).astype(BF16)


def token_back_body(experts, own_ref, got_ref, table_ref, got_table_ref, *refs):
    near, far, keep_ref, send_ref = refs[:experts], refs[experts : 2 * experts], refs[-2], refs[-1]
    rows = jnp.concatenate([own_ref[...], got_ref[...]], axis=0).astype(F32)
    columns = gate_columns(table_ref[...], got_table_ref[...], VALUE_GATE, VALUE_ROUTE)
    gated = gated_rows(experts, columns, rows)
    count, half = own_ref.shape[0], near[0].shape[0]
    for side, weights in enumerate((near, far)):
        total = None
        for i, right in enumerate(pair_up(weights)):
            left = jnp.concatenate(gated[2 * i : 2 * i + 2], axis=1)
            product = dot_nt(left, right)
            total = product if total is None else total + product
        keep_ref[:, side * half : (side + 1) * half] = total[:count]
        send_ref[:, side * half : (side + 1) * half] = total[count:].astype(BF16)


def attention_back_body(vr_ref, or_ref, table_ref, probs_ref, q_ref, k_ref, mixed_ref, hidden_ref, value_ref, head_ref, grad_ref, value_grad_ref, query_grad_ref, key_grad_ref, logit_ref):
    size = q_ref.shape[1]
    experts = logit_ref.shape[1] // 2
    probs = probs_ref[...]
    prob_grad = dot_nt(grad_ref[...], mixed_ref[...])
    score_grad = probs * (prob_grad - jnp.sum(prob_grad * probs, axis=1, keepdims=True))
    scaled = score_grad / math.sqrt(size)
    query_grad_ref[...] = dot(scaled.astype(BF16), k_ref[...]).astype(BF16)
    key_grad_ref[...] = dot(scaled.T.astype(BF16), q_ref[...]).astype(BF16)
    ids = lax.broadcasted_iota(jnp.int32, logit_ref.shape, 1)
    logit = jnp.zeros(logit_ref.shape, F32)
    hidden, value_grad = hidden_ref[...].astype(F32), value_grad_ref[...].astype(F32)
    for j in range(2):
        for gate_at, route, left, right, base in (
            (VALUE_GATE, vr_ref, value_grad, value_ref, 0),
            (OUTPUT_GATE, or_ref, hidden, head_ref, experts),
        ):
            gate = table_ref[:, gate_at + j : gate_at + j + 1]
            gate_grad = jnp.sum(
                left * right[:, j * size : (j + 1) * size].astype(F32), axis=1, keepdims=True
            )
            logit = jnp.where(
                ids == route[:, j : j + 1] + base, gate_grad * gate * (1.0 - gate), logit
            )
    logit_ref[...] = logit


def on_device(
    tokens,
    queries,
    key_vectors,
    gate_logits,
    value_routes,
    output_routes,
    value_weight,
    output_weight,
    cotangent,
):
    rows, features = tokens.shape
    size = queries.shape[1]
    experts = gate_logits.shape[1] // 2
    block = value_weight.shape[1]
    groups = lax.axis_size("dp")
    quads = groups // 4
    half = quads * block
    width = 2 * half
    at = lax.axis_index("dp")
    me = lax.axis_index("expert")

    def over_dp(x, flip):
        return lax.ppermute(x, "dp", [(i, i ^ flip) for i in range(groups)])

    def over_experts(x, flip):
        return lax.ppermute(x, "expert", [(i, i ^ flip) for i in range(experts)])

    def gather_weight(weight):
        own = weight[0]
        own = jnp.concatenate([own] + [over_dp(own, 4 * k) for k in range(1, quads)], axis=0)
        near = [own] + [over_experts(own, k) for k in range(1, experts)]
        return near, [over_dp(w, 1) for w in near]

    def feature_blocks(x, other):
        parts = []
        for core in range(2):
            for k in range(quads):
                start = (at ^ (4 * k + 2 * other + core)) * block
                parts.append(lax.dynamic_slice(x, (0, start), (rows, block)))
        return parts

    near_value, far_value = gather_weight(value_weight)
    near_output, far_output = gather_weight(output_weight)

    table, sent_table, probs, weights, weights_back = kernel_call(
        table_body,
        [((rows, 128), F32), ((rows, 128), BF16), ((rows, rows), F32), ((rows, rows), BF16), ((rows, rows), BF16)],
        me[None],
        gate_logits,
        value_routes,
        output_routes,
        queries,
        key_vectors,
        scalars=1,
    )
    got_table = over_dp(sent_table, 2)
    own_tokens = jnp.concatenate(feature_blocks(tokens, 0), axis=1)
    got_tokens = over_dp(jnp.concatenate(feature_blocks(tokens, 1), axis=1), 2)
    own_cotangent = jnp.concatenate(feature_blocks(cotangent, 0), axis=1)
    got_cotangent = over_dp(jnp.concatenate(feature_blocks(cotangent, 1), axis=1), 2)
    (turned_tokens,) = kernel_call(transpose_body, [((width, 2 * rows), BF16)], own_tokens, got_tokens)
    (turned_cotangent,) = kernel_call(
        transpose_body, [((width, 2 * rows), BF16)], own_cotangent, got_cotangent
    )

    product_flops = 2 * 2 * rows * width * experts * size

    def partial_products(own, got, near, far, gate, route):
        def body(*refs):
            partial_body(experts, gate, route, *refs)

        keep, send = kernel_call(
            body,
            [((rows, 2 * size), F32), ((rows, 2 * size), BF16)],
            own,
            got,
            table,
            got_table,
            *near,
            *far,
            flops=product_flops,
        )
        return keep, over_dp(send, 2)

    def weight_grad(turned, own, gate, route):
        got = over_dp(own, 2)

        def body(*refs):
            weight_grad_body(experts, gate, route, *refs)

        keep, send = kernel_call(
            body,
            [((experts, half, size), F32), ((experts, half, size), BF16)],
            turned,
            own,
            got,
            table,
            got_table,
            flops=product_flops,
        )
        sums = kernel_call(
            core_sum_body,
            [((half, size), F32)] + [((half, size), BF16)] * (experts - 1),
            keep,
            over_dp(send, 1),
        )
        total = sums[0]
        for k in range(1, experts):
            total = total + over_experts(sums[k], k).astype(F32)
        result = total[:block]
        for k in range(1, quads):
            sent = total[k * block : (k + 1) * block].astype(BF16)
            result = result + over_dp(sent, 4 * k).astype(F32)
        return (result / groups)[None], got

    value_parts = partial_products(own_tokens, got_tokens, near_value, far_value, VALUE_GATE, VALUE_ROUTE)
    expert_value, mixed_value, hidden = kernel_call(
        hidden_body,
        [((rows, 2 * size), BF16), ((rows, size), BF16), ((rows, size), BF16)],
        *value_parts,
        table,
        weights,
    )
    output_weight_grad, _ = weight_grad(turned_cotangent, hidden, OUTPUT_GATE, OUTPUT_ROUTE)

    head_parts = partial_products(
        own_cotangent, got_cotangent, near_output, far_output, OUTPUT_GATE, OUTPUT_ROUTE
    )
    head_back, hidden_grad, value_grad = kernel_call(
        head_body,
        [((rows, 2 * size), BF16), ((rows, size), BF16), ((rows, size), BF16)],
        *head_parts,
        table,
        weights_back,
    )
    value_weight_grad, got_value_grad = weight_grad(
        turned_tokens, value_grad, VALUE_GATE, VALUE_ROUTE
    )

    def back_body(*refs):
        token_back_body(experts, *refs)

    kept_back, sent_back = kernel_call(
        back_body,
        [((rows, width), F32), ((rows, width), BF16)],
        value_grad,
        got_value_grad,
        table,
        got_table,
        *near_value,
        *far_value,
        flops=product_flops,
    )
    parts = jnp.concatenate([kept_back.astype(BF16), over_dp(sent_back, 2)], axis=1)
    pieces = []
    for b in range(groups):
        flip = at ^ b
        place = ((flip >> 1) & 1) * 2 * quads + (flip & 1) * quads + (flip >> 2)
        pieces.append(lax.dynamic_slice(parts, (0, place * block), (rows, block)))
    token_grad = jnp.concatenate(pieces, axis=1)

    query_grad, key_grad, logit_grad = kernel_call(
        attention_back_body,
        [((rows, size), BF16), ((rows, size), BF16), ((rows, 2 * experts), F32)],
        value_routes,
        output_routes,
        table,
        probs,
        queries,
        key_vectors,
        mixed_value,
        hidden,
        expert_value,
        head_back,
        hidden_grad,
        value_grad,
    )
    return (token_grad, query_grad, key_grad, logit_grad, value_weight_grad, output_weight_grad)


def solution(mesh):
    rows, banks = P(("dp", "expert"), None), P("expert", "dp", None)
    return jax.shard_map(
        on_device,
        mesh=mesh,
        in_specs=(rows,) * 6 + (banks, banks, rows),
        out_specs=(rows,) * 4 + (banks, banks),
        check_vma=False,
    )
```

```python
import math

import jax
import jax.numpy as jnp
from jax import lax
from jax.experimental import pallas as pl
from jax.experimental.pallas import tpu as pltpu
from jax.sharding import PartitionSpec as P

F32, BF16 = jnp.float32, jnp.bfloat16
VALUE_GATE, OUTPUT_GATE, VALUE_ROUTE, OUTPUT_ROUTE, LOW_PART = 0, 2, 4, 6, 8


def kernel_call(body, outs, *args, scalars=0, flops=0, where=pltpu.VMEM, scratch=(), vmem=24):
    moved = sum(x.size * x.dtype.itemsize for x in args) + sum(
        math.prod(s) * jnp.dtype(t).itemsize for s, t in outs
    )
    return pl.pallas_call(
        body,
        out_shape=[jax.ShapeDtypeStruct(s, t) for s, t in outs],
        in_specs=[pl.BlockSpec(memory_space=pltpu.SMEM)] * scalars
        + [pl.BlockSpec(memory_space=where)] * (len(args) - scalars),
        out_specs=[pl.BlockSpec(memory_space=pltpu.VMEM)] * len(outs),
        cost_estimate=pl.CostEstimate(flops=flops, bytes_accessed=moved, transcendentals=0),
        scratch_shapes=list(scratch),
        compiler_params=pltpu.CompilerParams(vmem_limit_bytes=vmem * 2**20),
    )(*args)


def dot(left, right):
    return jnp.dot(left, right, preferred_element_type=F32)


def dot_nt(left, right):
    return lax.dot_general(left, right, (((1,), (1,)), ((), ())), preferred_element_type=F32)


def probs_body(q_ref, k_ref, probs_ref, weights_ref, back_ref):
    length = q_ref.shape[0]
    scores = dot_nt(q_ref[...], k_ref[...]) / math.sqrt(q_ref.shape[1])
    row_ids = lax.broadcasted_iota(jnp.int32, (length, length), 0)
    col_ids = lax.broadcasted_iota(jnp.int32, (length, length), 1)
    scores = jnp.where(row_ids >= col_ids, scores, -1e30)
    exponent = jnp.exp(scores - jnp.max(scores, axis=1, keepdims=True))
    probs = exponent / jnp.sum(exponent, axis=1, keepdims=True)
    probs_ref[...] = probs
    weights_ref[...] = probs.astype(BF16)
    back_ref[...] = probs.T.astype(BF16)


def token_table(me, logits, route_v, route_o):
    both, rows = logits.shape
    experts = both // 2
    gates = jax.nn.sigmoid(logits)
    ids = lax.broadcasted_iota(jnp.int32, (both, rows), 0)
    high, low = [], []
    for routes, first in ((route_v, 0), (route_o, experts)):
        for j in range(2):
            gate = jnp.sum(
                jnp.where(ids == routes[j : j + 1] + first, gates, 0.0), axis=0, keepdims=True
            )
            high.append(gate.astype(BF16).astype(F32))
            low.append(gate - high[-1])
    routes = [(routes ^ me).astype(F32) for routes in (route_v, route_o)]
    table = jnp.concatenate(high + routes + low, axis=0)
    return jnp.concatenate([table, jnp.zeros((128 - table.shape[0], rows), F32)], axis=0).T


def quad_table_body(column, *refs):
    out_ref = refs[-1]
    for i, ref in enumerate(refs[:-1]):
        rows = ref.shape[0]
        table = ref[:, column:].astype(F32)
        out_ref[i * rows : (i + 1) * rows, :] = jnp.concatenate(
            [
                table[:, :VALUE_ROUTE] + table[:, LOW_PART : LOW_PART + VALUE_ROUTE],
                table[:, VALUE_ROUTE:],
            ],
            axis=1,
        )


def pack_body(block, quads, at_ref, me_ref, tokens_ref, cotangent_ref, *refs):
    small_refs, out_refs, held_refs, sems = refs[:3], refs[3:7], refs[7:10], refs[10]
    copies = [
        pltpu.make_async_copy(ref, held, sems.at[i])
        for i, (ref, held) in enumerate(zip(small_refs, held_refs))
    ]
    for flip in (3, 2, 1, 0):
        for m, ref in enumerate((tokens_ref, cotangent_ref)):
            for k in range(quads):
                start = pl.multiple_of((at_ref[0] ^ (4 * k + flip)) * block, block)
                to = (m * quads + k) * block
                copies.append(
                    pltpu.make_async_copy(
                        ref.at[:, pl.ds(start, block)],
                        out_refs[flip].at[:, to : to + block],
                        sems.at[len(copies)],
                    )
                )
    for copy in copies:
        copy.start()
    for copy in copies[:3]:
        copy.wait()
    table = token_table(me_ref[0], *[held[...] for held in held_refs]).astype(BF16)
    for flip, out_ref in enumerate(out_refs):
        if flip != 2:
            out_ref[:, 2 * quads * block :] = table
    for copy in copies[3:]:
        copy.wait()


def table_body(me_ref, logits_ref, vr_ref, or_ref, out_ref):
    out_ref[...] = token_table(me_ref[0], logits_ref[...], vr_ref[...], or_ref[...]).astype(BF16)


def unpack_body(block, quads, at_ref, own_ref, core_ref, beside_ref, out_ref):
    half = quads * block
    for flip, (ref, first) in enumerate(
        ((own_ref, 0), (core_ref, 0), (beside_ref, 0), (beside_ref, half))
    ):
        for k in range(quads):
            start = pl.multiple_of((at_ref[0] ^ (4 * k + flip)) * block, block)
            out_ref[:, pl.ds(start, block)] = ref[:, first + k * block : first + (k + 1) * block]


def turn_body(*refs):
    out_ref = refs[-1]
    for i, ref in enumerate(refs[:-1]):
        rows = ref.shape[0]
        out_ref[:, i * rows : (i + 1) * rows] = ref[:, : out_ref.shape[0]].T


def turn_bank_body(experts, chunks, size, *refs):
    for e in range(experts):
        refs[-1][e * size : (e + 1) * size, :] = bank(refs[e * chunks : (e + 1) * chunks], 0).T


def bank(refs, side):
    return jnp.concatenate([ref[side] for ref in refs], axis=0)


def bank_pair(refs, chunks, side, i):
    return jnp.concatenate(
        [bank(refs[e * chunks : (e + 1) * chunks], side) for e in (i, i + 1)], axis=1
    )


def partial_body(experts, chunks, size, half, *refs):
    row_refs, table_ref, weights = refs[:4], refs[4], refs[5 : 5 + experts * chunks]
    keep_ref, send_ref = refs[-2:]
    count = row_refs[0].shape[0]
    for side, route in ((0, VALUE_ROUTE), (1, OUTPUT_ROUTE)):
        left = jnp.concatenate([r[:, side * half : (side + 1) * half] for r in row_refs], axis=0)
        routes = [table_ref[:, route + j : route + j + 1] for j in range(2)]
        slots = [jnp.zeros((4 * count, size), F32) for _ in range(2)]
        for i in range(0, experts, 2):
            product = dot(left, bank_pair(weights, chunks, side, i))
            for p in range(2):
                piece = product[:, p * size : (p + 1) * size]
                for j in range(2):
                    slots[j] = jnp.where(routes[j] == float(i + p), piece, slots[j])
        for j in range(2):
            lanes = slice((2 * side + j) * size, (2 * side + j + 1) * size)
            keep_ref[:, lanes] = slots[j][: 2 * count]
            send_ref[:, lanes] = slots[j][2 * count :].astype(BF16)


def core_sum_body(keep_ref, got_ref, own_ref, send_ref):
    count = own_ref.shape[0]
    own_ref[...] = keep_ref[:count] + got_ref[:count].astype(F32)
    send_ref[...] = (keep_ref[count:] + got_ref[count:].astype(F32)).astype(BF16)


def middle_body(keep_ref, got_ref, table_ref, weights_ref, back_ref, slots_ref, mixed_ref, grad_ref, sent_ref):
    count, size = mixed_ref.shape
    slots = (keep_ref[...] + got_ref[...].astype(F32)).astype(BF16)
    slots_ref[...] = slots
    gated = []
    for gate, base in ((VALUE_GATE, 0), (OUTPUT_GATE, 2)):
        total = jnp.zeros((count, size), F32)
        for j in range(2):
            rows = slots[:, (base + j) * size : (base + j + 1) * size].astype(F32)
            total += table_ref[:count, gate + j : gate + j + 1] * rows
        gated.append(total.astype(BF16))
    mixed_ref[...], grad_ref[...] = gated
    sent_ref[:, :size] = dot(weights_ref[...], gated[0]).astype(BF16)
    sent_ref[:, size:] = dot(back_ref[...], gated[1]).astype(BF16)


def gated_rows(experts, table_ref, gate, route, rows):
    gates = [table_ref[:, gate + j : gate + j + 1] for j in range(2)]
    routes = [table_ref[:, route + j : route + j + 1] for j in range(2)]
    gated = []
    for k in range(experts):
        column = sum(jnp.where(r == float(k), g, 0.0) for g, r in zip(gates, routes))
        gated.append((column * rows).astype(BF16))
    return gated


def weight_grad_body(experts, chunks, size, turned_ref, bank_ref, table_ref, *refs):
    row_refs, out_refs, back_refs = refs[:4], refs[4:-3], refs[-3:]
    half, count = turned_ref.shape[0] // 2, row_refs[0].shape[0]
    for side, gate, route, at in (
        (0, VALUE_GATE, VALUE_ROUTE, 1),
        (1, OUTPUT_GATE, OUTPUT_ROUTE, 0),
    ):
        rows = jnp.concatenate([r[:, at * size : (at + 1) * size] for r in row_refs], axis=0)
        gated = gated_rows(experts, table_ref, gate, route, rows.astype(F32))
        left = turned_ref[side * half : (side + 1) * half, :]
        for i in range(0, experts, 2):
            product = dot(left, jnp.concatenate(gated[i : i + 2], axis=1))
            for p in range(2):
                start = 0
                for out_ref in out_refs[(i + p) * chunks : (i + p + 1) * chunks]:
                    stop = start + out_ref.shape[1]
                    out_ref[side] = product[start:stop, p * size : (p + 1) * size].astype(
                        out_ref.dtype
                    )
                    start = stop
        if side == 0:
            back = dot(jnp.concatenate(gated, axis=1), bank_ref[...]).astype(BF16)
            back_refs[0][...], back_refs[1][...] = back[:count], back[count : 2 * count]
            back_refs[2][...] = back[2 * count :]


def merge_body(beside_ref, got_ref, own_ref, send_ref):
    count, half = beside_ref.shape
    own_ref[...] = got_ref[:count]
    send_ref[:, :half] = beside_ref[...]
    send_ref[:, half:] = got_ref[count:]


def chunk_sum_body(*refs):
    total = refs[0][...]
    for ref in refs[1:-1]:
        total += ref[...].astype(F32)
    refs[-1][...] = total.astype(BF16)


def final_sum_body(groups, *refs):
    total = refs[0][...]
    for ref in refs[1:-2]:
        total += ref[...].astype(F32)
    total = total / groups
    for side in range(2):
        refs[side - 2][0] = total[side]


def attention_back_body(vr_ref, or_ref, table_ref, probs_ref, q_ref, k_ref, mixed_ref, slots_ref, grad_ref, rows_ref, query_grad_ref, key_grad_ref, logit_ref):
    count, size = q_ref.shape
    both = logit_ref.shape[1]
    probs = probs_ref[...]
    prob_grad = dot_nt(grad_ref[...], mixed_ref[...])
    score_grad = probs * (prob_grad - jnp.sum(prob_grad * probs, axis=1, keepdims=True))
    scaled = score_grad / math.sqrt(size)
    query_grad_ref[...] = dot(scaled.astype(BF16), k_ref[...]).astype(BF16)
    key_grad_ref[...] = dot(scaled.T.astype(BF16), q_ref[...]).astype(BF16)
    ids = lax.broadcasted_iota(jnp.int32, (count, both), 1)
    logit = jnp.zeros((count, both), F32)
    for gate_at, route, at, base, first in (
        (VALUE_GATE, vr_ref, 1, 0, 0),
        (OUTPUT_GATE, or_ref, 0, 2, both // 2),
    ):
        rows = rows_ref[:, at * size : (at + 1) * size].astype(F32)
        for j in range(2):
            gate = table_ref[:count, gate_at + j : gate_at + j + 1]
            other = slots_ref[:, (base + j) * size : (base + j + 1) * size].astype(F32)
            gate_grad = jnp.sum(rows * other, axis=1, keepdims=True)
            logit = jnp.where(
                ids == route[:, j : j + 1] + first, gate_grad * gate * (1.0 - gate), logit
            )
    logit_ref[...] = logit


def on_device(
    tokens,
    queries,
    key_vectors,
    gate_logits,
    value_routes,
    output_routes,
    value_weight,
    output_weight,
    cotangent,
):
    count, features = tokens.shape
    size = queries.shape[1]
    experts = gate_logits.shape[1] // 2
    block = value_weight.shape[1]
    groups = lax.axis_size("dp")
    quads = groups // 4
    half = quads * block
    at = lax.axis_index("dp")
    me = lax.axis_index("expert")
    aligned = block % 128 == 0

    def over_dp(x, flip, what):
        with jax.named_scope(f"{what}_dp{flip}"):
            return lax.ppermute(x, "dp", [(i, i ^ flip) for i in range(groups)])

    def over_experts(x, flip, what):
        with jax.named_scope(f"{what}_expert{flip}"):
            return lax.ppermute(x, "expert", [(i, i ^ flip) for i in range(experts)])

    def side_by_side(arrays, axis):
        return arrays[0] if len(arrays) == 1 else jnp.concatenate(arrays, axis=axis)

    own_banks = jnp.concatenate([value_weight, output_weight], axis=0)
    other_banks = side_by_side([over_dp(own_banks, 4 * k, "banks") for k in range(1, quads)], 1)
    first_round = [over_experts(own_banks, k, "banks") for k in range(1, experts)]

    if aligned:
        packed = kernel_call(
            lambda *refs: pack_body(block, quads, *refs),
            [((count, 2 * half + (0 if flip == 2 else 128)), BF16) for flip in range(4)],
            at[None],
            me[None],
            tokens,
            cotangent,
            gate_logits.T,
            value_routes.T,
            output_routes.T,
            scalars=2,
            where=pl.ANY,
            scratch=[
                pltpu.VMEM((2 * experts, count), F32),
                pltpu.VMEM((2, count), jnp.int32),
                pltpu.VMEM((2, count), jnp.int32),
                pltpu.SemaphoreType.DMA((3 + 8 * quads,)),
            ],
            vmem=48,
        )
    else:
        (own_table,) = kernel_call(
            table_body,
            [((count, 128), BF16)],
            me[None],
            gate_logits.T,
            value_routes.T,
            output_routes.T,
            scalars=1,
        )
        packed = [
            jnp.concatenate(
                [
                    lax.dynamic_slice(x, (0, (at ^ (4 * k + flip)) * block), (count, block))
                    for x in (tokens, cotangent)
                    for k in range(quads)
                ]
                + ([] if flip == 2 else [own_table]),
                axis=1,
            )
            for flip in range(4)
        ]
    packed = list(packed)
    far_rows = over_dp(packed[3], 2, "far_rows")
    far_rows, other_banks, first_round, packed[2], packed[1] = lax.optimization_barrier(
        (far_rows, other_banks, first_round, packed[2], packed[1])
    )
    banks = [own_banks, other_banks]
    for k in range(1, experts):
        banks += [first_round[k - 1], over_experts(other_banks, k, "other_banks")]
    near_rows = over_dp(packed[2], 2, "near_rows")
    core_rows, core_far_rows = over_dp(packed[1], 1, "rows"), over_dp(far_rows, 1, "rows")
    rows = [packed[0], near_rows, core_rows, core_far_rows]
    (table,) = kernel_call(
        lambda *refs: quad_table_body(2 * half, *refs),
        [((4 * count, 128), F32)],
        packed[0],
        far_rows,
        core_rows,
        core_far_rows,
    )
    probs, weights, weights_back = kernel_call(
        probs_body,
        [((count, count), F32), ((count, count), BF16), ((count, count), BF16)],
        queries,
        key_vectors,
    )

    def from_quad(x, what):
        beside = over_dp(x, 2, what)
        return [x, beside, over_dp(x, 1, what), over_dp(beside, 1, what)]

    (turned_bank,) = kernel_call(
        lambda *refs: turn_bank_body(experts, 2, size, *refs), [((experts * size, half), BF16)], *banks
    )
    (turned,) = kernel_call(turn_body, [((2 * half, 4 * count), BF16)], *rows)

    product_flops = 2 * 4 * count * half * experts * size
    keep, send = kernel_call(
        lambda *refs: partial_body(experts, 2, size, half, *refs),
        [((2 * count, 4 * size), F32), ((2 * count, 4 * size), BF16)],
        *rows,
        table,
        *banks,
        flops=2 * product_flops,
    )
    keep, send = kernel_call(
        core_sum_body,
        [((count, 4 * size), F32), ((count, 4 * size), BF16)],
        keep,
        over_dp(send, 1, "partials"),
    )
    slots, mixed_value, hidden_grad, head_rows = kernel_call(
        middle_body,
        [((count, 4 * size), BF16), ((count, size), BF16), ((count, size), BF16), ((count, 2 * size), BF16)],
        keep,
        over_dp(send, 2, "partials"),
        table,
        weights,
        weights_back,
    )
    quad_rows = from_quad(head_rows, "head_rows")

    shapes = []
    for k in range(experts):
        kind = F32 if k == 0 else BF16
        shapes += [((2, block, size), kind), ((2, half - block, size), kind)]
    *grads, own_back, beside_back, core_back = kernel_call(
        lambda *refs: weight_grad_body(experts, 2, size, *refs),
        shapes + [((count, half), BF16), ((count, half), BF16), ((2 * count, half), BF16)],
        turned,
        turned_bank,
        table,
        *quad_rows,
        flops=3 * product_flops,
    )
    got_back, beside_back = kernel_call(
        merge_body,
        [((count, half), BF16), ((count, 2 * half), BF16)],
        beside_back,
        over_dp(core_back, 1, "token_back"),
    )
    back = [own_back, got_back, over_dp(beside_back, 2, "token_back")]

    def over_all_experts(chunk):
        return [grads[chunk]] + [
            over_experts(grads[2 * k + chunk], k, "grads") for k in range(1, experts)
        ]

    (others,) = kernel_call(
        chunk_sum_body, [((2, half - block, size), BF16)], *over_all_experts(1)
    )
    sums = over_all_experts(0) + [
        over_dp(others[:, (k - 1) * block : k * block], 4 * k, "grads") for k in range(1, quads)
    ]
    value_weight_grad, output_weight_grad = kernel_call(
        lambda *refs: final_sum_body(groups, *refs), [((1, block, size), F32)] * 2, *sums
    )

    if aligned:
        (token_grad,) = kernel_call(
            lambda *refs: unpack_body(block, quads, *refs),
            [((count, features), BF16)],
            at[None],
            *back,
            scalars=1,
        )
    else:
        back = jnp.concatenate(back, axis=1)
        token_grad = jnp.concatenate(
            [
                lax.dynamic_slice(
                    back,
                    (0, (((at ^ b) & 3) * quads + ((at ^ b) >> 2)) * block),
                    (count, block),
                )
                for b in range(groups)
            ],
            axis=1,
        )

    query_grad, key_grad, logit_grad = kernel_call(
        attention_back_body,
        [((count, size), BF16), ((count, size), BF16), ((count, 2 * experts), F32)],
        value_routes,
        output_routes,
        table,
        probs,
        queries,
        key_vectors,
        mixed_value,
        slots,
        hidden_grad,
        head_rows,
    )
    return (token_grad, query_grad, key_grad, logit_grad, value_weight_grad, output_weight_grad)


def solution(mesh):
    rows, banks = P(("dp", "expert"), None), P("expert", "dp", None)
    return jax.shard_map(
        on_device,
        mesh=mesh,
        in_specs=(rows,) * 6 + (banks, banks, rows),
        out_specs=(rows,) * 4 + (banks, banks),
        check_vma=False,
    )
```

```python
import math

import jax
import jax.numpy as jnp
from jax import lax
from jax.experimental import pallas as pl
from jax.experimental.pallas import tpu as pltpu
from jax.sharding import PartitionSpec as P

F32, BF16 = jnp.float32, jnp.bfloat16
VALUE_GATE, OUTPUT_GATE, VALUE_ROUTE, OUTPUT_ROUTE, LOW_PART = 0, 2, 4, 6, 8


def kernel_call(body, outs, *args, scalars=0, flops=0, where=pltpu.VMEM, scratch=(), vmem=24):
    moved = sum(x.size * x.dtype.itemsize for x in args) + sum(
        math.prod(s) * jnp.dtype(t).itemsize for s, t in outs
    )
    return pl.pallas_call(
        body,
        out_shape=[jax.ShapeDtypeStruct(s, t) for s, t in outs],
        in_specs=[pl.BlockSpec(memory_space=pltpu.SMEM)] * scalars
        + [pl.BlockSpec(memory_space=where)] * (len(args) - scalars),
        out_specs=[pl.BlockSpec(memory_space=pltpu.VMEM)] * len(outs),
        cost_estimate=pl.CostEstimate(flops=flops, bytes_accessed=moved, transcendentals=0),
        scratch_shapes=list(scratch),
        compiler_params=pltpu.CompilerParams(vmem_limit_bytes=vmem * 2**20),
    )(*args)


def dot(left, right):
    return jnp.dot(left, right, preferred_element_type=F32)


def dot_nt(left, right):
    return lax.dot_general(left, right, (((1,), (1,)), ((), ())), preferred_element_type=F32)


def probs_body(q_ref, k_ref, probs_ref, weights_ref):
    length = q_ref.shape[0]
    scores = dot_nt(q_ref[...], k_ref[...]) / math.sqrt(q_ref.shape[1])
    row_ids = lax.broadcasted_iota(jnp.int32, (length, length), 0)
    col_ids = lax.broadcasted_iota(jnp.int32, (length, length), 1)
    scores = jnp.where(row_ids >= col_ids, scores, -1e30)
    exponent = jnp.exp(scores - jnp.max(scores, axis=1, keepdims=True))
    probs = exponent / jnp.sum(exponent, axis=1, keepdims=True)
    probs_ref[...] = probs
    weights_ref[...] = probs.astype(BF16)


def token_table(me, logits, route_v, route_o):
    both, rows = logits.shape
    experts = both // 2
    gates = jax.nn.sigmoid(logits)
    ids = lax.broadcasted_iota(jnp.int32, (both, rows), 0)
    high, low = [], []
    for routes, first in ((route_v, 0), (route_o, experts)):
        for j in range(2):
            gate = jnp.sum(
                jnp.where(ids == routes[j : j + 1] + first, gates, 0.0), axis=0, keepdims=True
            )
            high.append(gate.astype(BF16).astype(F32))
            low.append(gate - high[-1])
    routes = [(routes ^ me).astype(F32) for routes in (route_v, route_o)]
    table = jnp.concatenate(high + routes + low, axis=0)
    return jnp.concatenate([table, jnp.zeros((128 - table.shape[0], rows), F32)], axis=0).T


def quad_table_body(column, *refs):
    out_ref = refs[-1]
    for i, ref in enumerate(refs[:-1]):
        rows = ref.shape[0]
        table = ref[:, column:].astype(F32)
        out_ref[i * rows : (i + 1) * rows, :] = jnp.concatenate(
            [
                table[:, :VALUE_ROUTE] + table[:, LOW_PART : LOW_PART + VALUE_ROUTE],
                table[:, VALUE_ROUTE:],
            ],
            axis=1,
        )


def pack_body(block, quads, at_ref, me_ref, tokens_ref, cotangent_ref, *refs):
    small_refs, out_refs, held_refs, sems = refs[:3], refs[3:7], refs[7:10], refs[10]
    copies = [
        pltpu.make_async_copy(ref, held, sems.at[i])
        for i, (ref, held) in enumerate(zip(small_refs, held_refs))
    ]
    for flip in (3, 2, 1, 0):
        for m, ref in enumerate((tokens_ref, cotangent_ref)):
            for k in range(quads):
                start = pl.multiple_of((at_ref[0] ^ (4 * k + flip)) * block, block)
                to = (m * quads + k) * block
                copies.append(
                    pltpu.make_async_copy(
                        ref.at[:, pl.ds(start, block)],
                        out_refs[flip].at[:, to : to + block],
                        sems.at[len(copies)],
                    )
                )
    for copy in copies:
        copy.start()
    for copy in copies[:3]:
        copy.wait()
    table = token_table(me_ref[0], *[held[...] for held in held_refs]).astype(BF16)
    for flip, out_ref in enumerate(out_refs):
        if flip != 2:
            out_ref[:, 2 * quads * block :] = table
    for copy in copies[3:]:
        copy.wait()


def table_body(me_ref, logits_ref, vr_ref, or_ref, out_ref):
    out_ref[...] = token_table(me_ref[0], logits_ref[...], vr_ref[...], or_ref[...]).astype(BF16)


def unpack_body(block, quads, at_ref, own_ref, core_ref, beside_ref, out_ref):
    half = quads * block
    for flip, (ref, first) in enumerate(
        ((own_ref, 0), (core_ref, 0), (beside_ref, 0), (beside_ref, half))
    ):
        for k in range(quads):
            start = pl.multiple_of((at_ref[0] ^ (4 * k + flip)) * block, block)
            out_ref[:, pl.ds(start, block)] = ref[
                : out_ref.shape[0], first + k * block : first + (k + 1) * block
            ]


def turn_body(*refs):
    out_ref = refs[-1]
    for i, ref in enumerate(refs[:-1]):
        rows = ref.shape[0]
        out_ref[:, i * rows : (i + 1) * rows] = ref[:, : out_ref.shape[0]].T


def turn_bank_body(experts, chunks, size, *refs):
    for e in range(experts):
        refs[-1][e * size : (e + 1) * size, :] = bank(refs[e * chunks : (e + 1) * chunks], 0).T


def bank(refs, side):
    return jnp.concatenate([ref[side] for ref in refs], axis=0)


def bank_pair(refs, chunks, side, i):
    return jnp.concatenate(
        [bank(refs[e * chunks : (e + 1) * chunks], side) for e in (i, i + 1)], axis=1
    )


def partial_body(experts, chunks, size, half, *refs):
    row_refs, table_ref, weights = refs[:4], refs[4], refs[5 : 5 + experts * chunks]
    slots_ref, keep_ref, send_ref = refs[-3:]
    count = row_refs[0].shape[0]
    for side, gate, route in ((0, VALUE_GATE, VALUE_ROUTE), (1, OUTPUT_GATE, OUTPUT_ROUTE)):
        left = jnp.concatenate([r[:, side * half : (side + 1) * half] for r in row_refs], axis=0)
        routes = [table_ref[:, route + j : route + j + 1] for j in range(2)]
        slots = [jnp.zeros((4 * count, size), F32) for _ in range(2)]
        for i in range(0, experts, 2):
            product = dot(left, bank_pair(weights, chunks, side, i))
            for p in range(2):
                piece = product[:, p * size : (p + 1) * size]
                for j in range(2):
                    slots[j] = jnp.where(routes[j] == float(i + p), piece, slots[j])
        mixed = sum(table_ref[:, gate + j : gate + j + 1] * slots[j] for j in range(2))
        for j in range(2):
            slots_ref[:, (2 * side + j) * size : (2 * side + j + 1) * size] = slots[j].astype(BF16)
        lanes = slice(side * size, (side + 1) * size)
        keep_ref[:, lanes] = mixed[: 2 * count]
        send_ref[:, lanes] = mixed[2 * count :].astype(BF16)


def core_sum_body(keep_ref, got_ref, weights_ref, sum_ref, send_ref):
    both, count = keep_ref.shape[0], weights_ref.shape[0]
    total = keep_ref[...] + got_ref[...].astype(F32)
    sum_ref[...] = total
    send_ref[:both, :] = total.astype(BF16)
    send_ref[both:, :count] = weights_ref[: count // 2, :]
    send_ref[both:, count:] = weights_ref[count // 2 :, :]


def middle_body(sum_ref, got_ref, weights_ref, mixed_ref, grad_ref, rows_ref):
    count, size = mixed_ref.shape
    far_weights = jnp.concatenate(
        [got_ref[2 * count :, :count], got_ref[2 * count :, count:]], axis=0
    )
    for i, weights in enumerate((weights_ref[...], far_weights)):
        total = sum_ref[i * count : (i + 1) * count, :] + got_ref[
            (1 - i) * count : (2 - i) * count, :
        ].astype(F32)
        total = total.astype(BF16)
        if i == 0:
            mixed_ref[...], grad_ref[...] = total[:, :size], total[:, size:]
        rows_ref[i * count : (i + 1) * count, :size] = dot(weights, total[:, :size]).astype(BF16)
        rows_ref[i * count : (i + 1) * count, size:] = lax.dot_general(
            weights, total[:, size:], (((0,), (0,)), ((), ())), preferred_element_type=F32
        ).astype(BF16)


def two_parts(columns):
    rows = columns[0].shape[0]
    lane = lax.broadcasted_iota(jnp.int32, (rows, 128), 1)
    block = jnp.zeros((rows, 128), F32)
    for j, column in enumerate(columns):
        high = column.astype(BF16).astype(F32)
        block = jnp.where(lane == j, high, block)
        block = jnp.where(lane == 4 + j, column - high, block)
    return block.astype(BF16)


def whole_columns(block):
    block = block.astype(F32)
    return [block[:, j : j + 1] + block[:, 4 + j : 5 + j] for j in range(4)]


def gated_rows(experts, table_ref, gate, route, rows):
    gates = [table_ref[:, gate + j : gate + j + 1] for j in range(2)]
    routes = [table_ref[:, route + j : route + j + 1] for j in range(2)]
    gated = []
    for k in range(experts):
        column = sum(jnp.where(r == float(k), g, 0.0) for g, r in zip(gates, routes))
        gated.append((column * rows).astype(BF16))
    return gated


def weight_grad_body(experts, chunks, size, turned_ref, bank_ref, table_ref, slots_ref, *refs):
    row_refs, out_refs, back_refs = refs[:2], refs[2:-3], refs[-3:]
    half, count = turned_ref.shape[0] // 2, row_refs[0].shape[0] // 2
    gate_grads = []
    for side, gate, route, at in (
        (0, VALUE_GATE, VALUE_ROUTE, 1),
        (1, OUTPUT_GATE, OUTPUT_ROUTE, 0),
    ):
        rows = jnp.concatenate([r[:, at * size : (at + 1) * size] for r in row_refs], axis=0)
        rows = rows.astype(F32)
        gated = gated_rows(experts, table_ref, gate, route, rows)
        left = turned_ref[side * half : (side + 1) * half, :]
        for i in range(0, experts, 2):
            product = dot(left, jnp.concatenate(gated[i : i + 2], axis=1))
            for p in range(2):
                start = 0
                for out_ref in out_refs[(i + p) * chunks : (i + p + 1) * chunks]:
                    stop = start + out_ref.shape[1]
                    out_ref[side] = product[start:stop, p * size : (p + 1) * size].astype(
                        out_ref.dtype
                    )
                    start = stop
        if side == 0:
            back = dot(jnp.concatenate(gated, axis=1), bank_ref[...]).astype(BF16)
        for j in range(2):
            slot = slots_ref[:, (2 * side + j) * size : (2 * side + j + 1) * size].astype(F32)
            gate_grads.append(jnp.sum(rows * slot, axis=1, keepdims=True))
    gate_block = two_parts(gate_grads)
    for i, back_ref in enumerate(back_refs):
        start, stop = (i * count, (i + 1) * count) if i < 2 else (2 * count, 4 * count)
        back_ref[:, :half] = back[start:stop]
        back_ref[:, half:] = gate_block[start:stop]


def merge_body(own_ref, beside_ref, got_ref, gate_ref, send_ref):
    count, half = beside_ref.shape[0], beside_ref.shape[1] - 128
    sums = [
        two_parts(
            [
                near + far
                for near, far in zip(whole_columns(ref[:, half:]), whole_columns(got))
            ]
        )
        for ref, got in ((own_ref, got_ref[:count, half:]), (beside_ref, got_ref[count:, half:]))
    ]
    gate_ref[...] = sums[0]
    send_ref[:, :half] = beside_ref[:, :half]
    send_ref[:, half : 2 * half] = got_ref[count:, :half]
    send_ref[:, 2 * half :] = sums[1]


def logit_body(gate_ref, got_ref, table_ref, vr_ref, or_ref, out_ref):
    both, count = out_ref.shape
    got = got_ref[:, got_ref.shape[1] - 128 :]
    near, far = gate_ref[...].astype(F32).T, got.astype(F32).T
    gates = table_ref[:count, :].T
    ids = lax.broadcasted_iota(jnp.int32, (both, count), 0)
    logit = jnp.zeros((both, count), F32)
    for side, (route_ref, first) in enumerate(((vr_ref, 0), (or_ref, both // 2))):
        for j in range(2):
            at = 2 * side + j
            grad = (near[at : at + 1] + near[4 + at : 5 + at]) + (
                far[at : at + 1] + far[4 + at : 5 + at]
            )
            gate = gates[at : at + 1]
            logit = jnp.where(
                ids == route_ref[j : j + 1, :] + first, grad * gate * (1.0 - gate), logit
            )
    out_ref[...] = logit


def chunk_sum_body(*refs):
    total = refs[0][...]
    for ref in refs[1:-1]:
        total += ref[...].astype(F32)
    refs[-1][...] = total.astype(BF16)


def final_sum_body(groups, *refs):
    total = refs[0][...]
    for ref in refs[1:-2]:
        total += ref[...].astype(F32)
    total = total / groups
    for side in range(2):
        refs[side - 2][0] = total[side]


def attention_back_body(probs_ref, q_ref, k_ref, mixed_ref, grad_ref, query_grad_ref, key_grad_ref):
    probs = probs_ref[...]
    prob_grad = dot_nt(grad_ref[...], mixed_ref[...])
    score_grad = probs * (prob_grad - jnp.sum(prob_grad * probs, axis=1, keepdims=True))
    scaled = score_grad / math.sqrt(q_ref.shape[1])
    query_grad_ref[...] = dot(scaled.astype(BF16), k_ref[...]).astype(BF16)
    key_grad_ref[...] = dot(scaled.T.astype(BF16), q_ref[...]).astype(BF16)


def on_device(
    tokens,
    queries,
    key_vectors,
    gate_logits,
    value_routes,
    output_routes,
    value_weight,
    output_weight,
    cotangent,
):
    count, features = tokens.shape
    size = queries.shape[1]
    experts = gate_logits.shape[1] // 2
    block = value_weight.shape[1]
    groups = lax.axis_size("dp")
    quads = groups // 4
    half = quads * block
    at = lax.axis_index("dp")
    me = lax.axis_index("expert")
    aligned = block % 128 == 0

    def over_dp(x, flip, what):
        with jax.named_scope(f"{what}_dp{flip}"):
            return lax.ppermute(x, "dp", [(i, i ^ flip) for i in range(groups)])

    def over_experts(x, flip, what):
        with jax.named_scope(f"{what}_expert{flip}"):
            return lax.ppermute(x, "expert", [(i, i ^ flip) for i in range(experts)])

    def side_by_side(arrays, axis):
        return arrays[0] if len(arrays) == 1 else jnp.concatenate(arrays, axis=axis)

    own_banks = jnp.concatenate([value_weight, output_weight], axis=0)
    first_round = [over_experts(own_banks, k, "banks") for k in range(1, experts)]
    other_banks = side_by_side([over_dp(own_banks, 4 * k, "banks") for k in range(1, quads)], 1)

    if aligned:
        packed = kernel_call(
            lambda *refs: pack_body(block, quads, *refs),
            [((count, 2 * half + (0 if flip == 2 else 128)), BF16) for flip in range(4)],
            at[None],
            me[None],
            tokens,
            cotangent,
            gate_logits.T,
            value_routes.T,
            output_routes.T,
            scalars=2,
            where=pl.ANY,
            scratch=[
                pltpu.VMEM((2 * experts, count), F32),
                pltpu.VMEM((2, count), jnp.int32),
                pltpu.VMEM((2, count), jnp.int32),
                pltpu.SemaphoreType.DMA((3 + 8 * quads,)),
            ],
            vmem=60,
        )
    else:
        (own_table,) = kernel_call(
            table_body,
            [((count, 128), BF16)],
            me[None],
            gate_logits.T,
            value_routes.T,
            output_routes.T,
            scalars=1,
        )
        packed = [
            jnp.concatenate(
                [
                    lax.dynamic_slice(x, (0, (at ^ (4 * k + flip)) * block), (count, block))
                    for x in (tokens, cotangent)
                    for k in range(quads)
                ]
                + ([] if flip == 2 else [own_table]),
                axis=1,
            )
            for flip in range(4)
        ]
    packed = list(packed)
    far_rows = over_dp(packed[3], 2, "far_rows")
    far_rows, first_round, other_banks, packed[2], packed[1] = lax.optimization_barrier(
        (far_rows, first_round, other_banks, packed[2], packed[1])
    )
    banks = [own_banks, other_banks]
    for k in range(1, experts):
        banks += [first_round[k - 1], over_experts(other_banks, k, "other_banks")]
    near_rows = over_dp(packed[2], 2, "near_rows")
    core_rows, core_far_rows = over_dp(packed[1], 1, "rows"), over_dp(far_rows, 1, "rows")
    rows = [packed[0], near_rows, core_rows, core_far_rows]
    (table,) = kernel_call(
        lambda *refs: quad_table_body(2 * half, *refs),
        [((4 * count, 128), F32)],
        packed[0],
        far_rows,
        core_rows,
        core_far_rows,
    )
    probs, weights = kernel_call(
        probs_body,
        [((count, count), F32), ((count, count), BF16)],
        queries,
        key_vectors,
    )

    (turned_bank,) = kernel_call(
        lambda *refs: turn_bank_body(experts, 2, size, *refs), [((experts * size, half), BF16)], *banks
    )
    (turned,) = kernel_call(turn_body, [((2 * half, 4 * count), BF16)], *rows)

    product_flops = 2 * 4 * count * half * experts * size
    slots, keep, send = kernel_call(
        lambda *refs: partial_body(experts, 2, size, half, *refs),
        [((4 * count, 4 * size), BF16), ((2 * count, 2 * size), F32), ((2 * count, 2 * size), BF16)],
        *rows,
        table,
        *banks,
        flops=2 * product_flops,
    )
    chip_sum, send = kernel_call(
        core_sum_body,
        [((2 * count, 2 * size), F32), ((2 * count + count // 2, 2 * size), BF16)],
        keep,
        over_dp(send, 1, "partials"),
        weights,
    )
    got_sum, turned, turned_bank = lax.optimization_barrier(
        (over_dp(send, 2, "partials"), turned, turned_bank)
    )
    mixed_value, hidden_grad, head_rows = kernel_call(
        middle_body,
        [((count, size), BF16), ((count, size), BF16), ((2 * count, 2 * size), BF16)],
        chip_sum,
        got_sum,
        weights,
    )

    shapes = []
    for k in range(experts):
        kind = F32 if k == 0 else BF16
        shapes += [((2, block, size), kind), ((2, half - block, size), kind)]
    *grads, own_back, beside_back, core_back = kernel_call(
        lambda *refs: weight_grad_body(experts, 2, size, *refs),
        shapes + [((n * count, half + 128), BF16) for n in (1, 1, 2)],
        turned,
        turned_bank,
        table,
        slots,
        head_rows,
        over_dp(head_rows, 1, "head_rows"),
        flops=3 * product_flops,
    )
    def over_all_experts(chunk):
        return [grads[chunk]] + [
            over_experts(grads[2 * k + chunk], k, "grads") for k in range(1, experts)
        ]

    far_chunk = over_all_experts(1)
    got_back = over_dp(core_back, 1, "token_back")
    gate_sums, beside_back = kernel_call(
        merge_body,
        [((count, 128), BF16), ((count, 2 * half + 128), BF16)],
        own_back,
        beside_back,
        got_back,
    )
    back = [own_back, got_back, over_dp(beside_back, 2, "token_back")]

    (others,) = kernel_call(
        chunk_sum_body, [((2, half - block, size), BF16)], *far_chunk, flops=10**9
    )
    sums = over_all_experts(0) + [
        over_dp(others[:, (k - 1) * block : k * block], 4 * k, "grads") for k in range(1, quads)
    ]

    if aligned:
        (token_grad,) = kernel_call(
            lambda *refs: unpack_body(block, quads, *refs),
            [((count, features), BF16)],
            at[None],
            *back,
            scalars=1,
        )
    else:
        parts = jnp.concatenate(
            [back[0][:, :half], back[1][:count, :half], back[2][:, : 2 * half]], axis=1
        )
        token_grad = jnp.concatenate(
            [
                lax.dynamic_slice(
                    parts,
                    (0, (((at ^ b) & 3) * quads + ((at ^ b) >> 2)) * block),
                    (count, block),
                )
                for b in range(groups)
            ],
            axis=1,
        )

    (logit_grad,) = kernel_call(
        logit_body,
        [((2 * experts, count), F32)],
        gate_sums,
        back[2],
        table,
        value_routes.T,
        output_routes.T,
    )
    token_grad, logit_grad, sums = lax.optimization_barrier((token_grad, logit_grad, sums))
    value_weight_grad, output_weight_grad = kernel_call(
        lambda *refs: final_sum_body(groups, *refs), [((1, block, size), F32)] * 2, *sums
    )

    query_grad, key_grad = kernel_call(
        attention_back_body,
        [((count, size), BF16), ((count, size), BF16)],
        probs,
        queries,
        key_vectors,
        mixed_value,
        hidden_grad,
    )
    return (token_grad, query_grad, key_grad, logit_grad.T, value_weight_grad, output_weight_grad)


def solution(mesh):
    rows, banks = P(("dp", "expert"), None), P("expert", "dp", None)
    return jax.shard_map(
        on_device,
        mesh=mesh,
        in_specs=(rows,) * 6 + (banks, banks, rows),
        out_specs=(rows,) * 4 + (banks, banks),
        check_vma=False,
    )
```

```python
import math

import jax
import jax.numpy as jnp
from jax import lax
from jax.experimental import pallas as pl
from jax.experimental.pallas import tpu as pltpu
from jax.sharding import PartitionSpec as P

F32, BF16 = jnp.float32, jnp.bfloat16
VALUE_GATE, OUTPUT_GATE, VALUE_ROUTE, OUTPUT_ROUTE, LOW_PART, DENSE = 0, 2, 4, 6, 8, 16


def kernel_call(body, outs, *args, scalars=0, flops=0, moved=None, where=pltpu.VMEM, scratch=(), vmem=24):
    moved = moved or sum(x.size * x.dtype.itemsize for x in args) + sum(
        math.prod(s) * jnp.dtype(t).itemsize for s, t in outs
    )
    return pl.pallas_call(
        body,
        out_shape=[jax.ShapeDtypeStruct(s, t) for s, t in outs],
        in_specs=[pl.BlockSpec(memory_space=pltpu.SMEM)] * scalars
        + [pl.BlockSpec(memory_space=where)] * (len(args) - scalars),
        out_specs=[pl.BlockSpec(memory_space=pltpu.VMEM)] * len(outs),
        cost_estimate=pl.CostEstimate(flops=flops, bytes_accessed=moved, transcendentals=0),
        scratch_shapes=list(scratch),
        compiler_params=pltpu.CompilerParams(vmem_limit_bytes=vmem * 2**20),
    )(*args)


def dot(left, right):
    return jnp.dot(left, right, preferred_element_type=F32)


def dot_nt(left, right):
    return lax.dot_general(left, right, (((1,), (1,)), ((), ())), preferred_element_type=F32)


def probs_body(q_ref, k_ref, probs_ref, weights_ref):
    length = q_ref.shape[0]
    scores = dot_nt(q_ref[...], k_ref[...]) / math.sqrt(q_ref.shape[1])
    row_ids = lax.broadcasted_iota(jnp.int32, (length, length), 0)
    col_ids = lax.broadcasted_iota(jnp.int32, (length, length), 1)
    scores = jnp.where(row_ids >= col_ids, scores, -1e30)
    exponent = jnp.exp(scores - jnp.max(scores, axis=1, keepdims=True))
    probs = exponent / jnp.sum(exponent, axis=1, keepdims=True)
    probs_ref[...] = probs
    weights_ref[...] = probs.astype(BF16)


def token_table(me, logits, route_v, route_o):
    both, rows = logits.shape
    experts = both // 2
    gates = jax.nn.sigmoid(logits)
    ids = lax.broadcasted_iota(jnp.int32, (both, rows), 0)
    high, low = [], []
    for routes, first in ((route_v, 0), (route_o, experts)):
        for j in range(2):
            gate = jnp.sum(
                jnp.where(ids == routes[j : j + 1] + first, gates, 0.0), axis=0, keepdims=True
            )
            high.append(gate.astype(BF16).astype(F32))
            low.append(gate - high[-1])
    routes = [(routes ^ me).astype(F32) for routes in (route_v, route_o)]
    table = jnp.concatenate(high + routes + low, axis=0)
    return jnp.concatenate([table, jnp.zeros((128 - table.shape[0], rows), F32)], axis=0).T


def quad_table_body(experts, *refs):
    out_ref = refs[-1]
    for i, ref in enumerate(refs[:-1]):
        rows = ref.shape[0]
        table = ref[:, ref.shape[1] - 128 :].astype(F32)
        gates = table[:, :VALUE_ROUTE] + table[:, LOW_PART : LOW_PART + VALUE_ROUTE]
        lane = lax.broadcasted_iota(jnp.int32, (rows, 128), 1).astype(F32)
        table = jnp.concatenate([gates, table[:, VALUE_ROUTE:LOW_PART], table[:, LOW_PART:]], axis=1)
        for gate, route, first in (
            (VALUE_GATE, VALUE_ROUTE, DENSE),
            (OUTPUT_GATE, OUTPUT_ROUTE, DENSE + experts),
        ):
            for j in range(2):
                at = table[:, route + j : route + j + 1] + float(first)
                table = jnp.where(lane == at, table[:, gate + j : gate + j + 1], table)
        out_ref[i * rows : (i + 1) * rows, :] = table


def pack_body(block, quads, groups, at_ref, me_ref, tokens_ref, cotangent_ref, value_ref, output_ref, *refs):
    small_refs, bank_ref, out_refs, held_refs, sems = refs[:3], refs[3], refs[4:7], refs[7:10], refs[10]
    small = [
        pltpu.make_async_copy(ref, held, sems.at[i])
        for i, (ref, held) in enumerate(zip(small_refs, held_refs))
    ]
    copies = [
        pltpu.make_async_copy(ref.at[0], bank_ref.at[i], sems.at[3 + i])
        for i, ref in enumerate((value_ref, output_ref))
    ]
    for group, out_ref in zip(groups, out_refs):
        to = 0
        for flip in group:
            for ref in (tokens_ref, cotangent_ref):
                for k in range(quads):
                    start = pl.multiple_of((at_ref[0] ^ (4 * k + flip)) * block, block)
                    copies.append(
                        pltpu.make_async_copy(
                            ref.at[:, pl.ds(start, block)],
                            out_ref.at[:, to : to + block],
                            sems.at[3 + len(copies)],
                        )
                    )
                    to += block
    for copy in small + copies:
        copy.start()
    for copy in small:
        copy.wait()
    table = token_table(me_ref[0], *[held[...] for held in held_refs]).astype(BF16)
    for out_ref in out_refs:
        out_ref[:, out_ref.shape[1] - 128 :] = table
    for copy in copies:
        copy.wait()


def table_body(me_ref, logits_ref, vr_ref, or_ref, out_ref):
    out_ref[...] = token_table(me_ref[0], logits_ref[...], vr_ref[...], or_ref[...]).astype(BF16)


def unpack_body(block, quads, at_ref, own_ref, core_ref, beside_ref, out_ref):
    half = quads * block
    for flip, (ref, first) in enumerate(
        ((own_ref, 0), (core_ref, 0), (beside_ref, 0), (beside_ref, half))
    ):
        for k in range(quads):
            start = pl.multiple_of((at_ref[0] ^ (4 * k + flip)) * block, block)
            out_ref[:, pl.ds(start, block)] = ref[
                : out_ref.shape[0], first + k * block : first + (k + 1) * block
            ]


def turn_body(*refs):
    out_ref = refs[-1]
    for i, ref in enumerate(refs[:-1]):
        rows = ref.shape[0]
        out_ref[:, i * rows : (i + 1) * rows] = ref[:, : out_ref.shape[0]].T


def copy_body(in_ref, out_ref):
    out_ref[...] = in_ref[...]


def tail_body(in_ref, out_ref):
    out_ref[...] = in_ref[:, in_ref.shape[1] - out_ref.shape[1] :]


def turn_bank_body(size, *refs):
    for e, ref in enumerate(refs[:-1]):
        refs[-1][e * size : (e + 1) * size, :] = ref[0].T


def bank(refs, side):
    return jnp.concatenate([ref[side] for ref in refs], axis=0)


def bank_pair(refs, chunks, side, i):
    return jnp.concatenate(
        [bank(refs[e * chunks : (e + 1) * chunks], side) for e in (i, i + 1)], axis=1
    )


def expert_products(experts, chunks, half, side, row_refs, weights):
    left = jnp.concatenate([r[:, side * half : (side + 1) * half] for r in row_refs], axis=0)
    for i in range(0, experts, 2):
        product = dot(left, bank_pair(weights, chunks, side, i))
        size = product.shape[1] // 2
        yield i, product[:, :size]
        yield i + 1, product[:, size:]


def partial_body(experts, chunks, size, half, *refs):
    row_refs, table_ref, weights = refs[:4], refs[4], refs[5 : 5 + experts * chunks]
    keep_ref, send_ref = refs[-2:]
    count = row_refs[0].shape[0]
    for side in range(2):
        mixed = jnp.zeros((4 * count, size), F32)
        for e, product in expert_products(experts, chunks, half, side, row_refs, weights):
            at = DENSE + side * experts + e
            mixed += table_ref[:, at : at + 1] * product
        lanes = slice(side * size, (side + 1) * size)
        keep_ref[:, lanes] = mixed[: 2 * count]
        send_ref[:, lanes] = mixed[2 * count :].astype(BF16)


def slots_body(experts, chunks, size, half, *refs):
    row_refs, table_ref, weights = refs[:4], refs[4], refs[5 : 5 + experts * chunks]
    slots_ref = refs[-1]
    count = row_refs[0].shape[0]
    for side, route in ((0, VALUE_ROUTE), (1, OUTPUT_ROUTE)):
        routes = [table_ref[:, route + j : route + j + 1] for j in range(2)]
        slots = [jnp.zeros((4 * count, size), F32) for _ in range(2)]
        for e, product in expert_products(experts, chunks, half, side, row_refs, weights):
            for j in range(2):
                slots[j] = jnp.where(routes[j] == float(e), product, slots[j])
        for j in range(2):
            slots_ref[:, (2 * side + j) * size : (2 * side + j + 1) * size] = slots[j].astype(BF16)


def core_sum_body(keep_ref, got_ref, weights_ref, sum_ref, send_ref):
    both, count = keep_ref.shape[0], weights_ref.shape[0]
    total = keep_ref[...] + got_ref[...].astype(F32)
    sum_ref[...] = total
    send_ref[:both, :] = total.astype(BF16)
    send_ref[both:, :count] = weights_ref[: count // 2, :]
    send_ref[both:, count:] = weights_ref[count // 2 :, :]


def middle_body(sum_ref, got_ref, weights_ref, mixed_ref, grad_ref, rows_ref):
    count, size = mixed_ref.shape
    far_weights = jnp.concatenate(
        [got_ref[2 * count :, :count], got_ref[2 * count :, count:]], axis=0
    )
    for i, weights in enumerate((weights_ref[...], far_weights)):
        total = sum_ref[i * count : (i + 1) * count, :] + got_ref[
            (1 - i) * count : (2 - i) * count, :
        ].astype(F32)
        total = total.astype(BF16)
        if i == 0:
            mixed_ref[...], grad_ref[...] = total[:, :size], total[:, size:]
        rows_ref[i * count : (i + 1) * count, :size] = dot(weights, total[:, :size]).astype(BF16)
        rows_ref[i * count : (i + 1) * count, size:] = lax.dot_general(
            weights, total[:, size:], (((0,), (0,)), ((), ())), preferred_element_type=F32
        ).astype(BF16)


def two_parts(columns):
    rows = columns[0].shape[0]
    lane = lax.broadcasted_iota(jnp.int32, (rows, 128), 1)
    block = jnp.zeros((rows, 128), F32)
    for j, column in enumerate(columns):
        high = column.astype(BF16).astype(F32)
        block = jnp.where(lane == j, high, block)
        block = jnp.where(lane == 4 + j, column - high, block)
    return block.astype(BF16)


def whole_columns(block):
    block = block.astype(F32)
    return [block[:, j : j + 1] + block[:, 4 + j : 5 + j] for j in range(4)]


def gated_rows(experts, side, table_ref, rows):
    first = DENSE + side * experts
    return [
        (table_ref[:, e : e + 1] * rows).astype(BF16) for e in range(first, first + experts)
    ]


def weight_grad_body(experts, chunks, size, turned_ref, *refs):
    bank_refs, (table_ref, slots_ref), refs = refs[:2], refs[2:4], refs[4:]
    row_refs, out_refs, back_refs = refs[:2], refs[2:-3], refs[-3:]
    half, count = turned_ref.shape[0] // 2, row_refs[0].shape[0] // 2
    gate_grads = []
    for side, at in ((0, 1), (1, 0)):
        rows = jnp.concatenate([r[:, at * size : (at + 1) * size] for r in row_refs], axis=0)
        rows = rows.astype(F32)
        gated = gated_rows(experts, side, table_ref, rows)
        left = turned_ref[side * half : (side + 1) * half, :]
        for i in range(0, experts, 2):
            product = dot(left, jnp.concatenate(gated[i : i + 2], axis=1))
            for p in range(2):
                start = 0
                for out_ref in out_refs[(i + p) * chunks : (i + p + 1) * chunks]:
                    stop = start + out_ref.shape[1]
                    out_ref[side] = product[start:stop, p * size : (p + 1) * size].astype(
                        out_ref.dtype
                    )
                    start = stop
        if side == 0:
            bank_rows = jnp.concatenate([ref[...] for ref in bank_refs], axis=1)
            back = dot(jnp.concatenate(gated, axis=1), bank_rows).astype(BF16)
        for j in range(2):
            slot = slots_ref[:, (2 * side + j) * size : (2 * side + j + 1) * size].astype(F32)
            gate_grads.append(jnp.sum(rows * slot, axis=1, keepdims=True))
    gate_block = two_parts(gate_grads)
    for i, back_ref in enumerate(back_refs):
        start, stop = (i * count, (i + 1) * count) if i < 2 else (2 * count, 4 * count)
        back_ref[:, :half] = back[start:stop]
        back_ref[:, half:] = gate_block[start:stop]


def merge_body(own_ref, beside_ref, got_ref, gate_ref, send_ref):
    count, half = beside_ref.shape[0], beside_ref.shape[1] - 128
    sums = [
        two_parts(
            [
                near + far
                for near, far in zip(whole_columns(ref[:, half:]), whole_columns(got))
            ]
        )
        for ref, got in ((own_ref, got_ref[:count, half:]), (beside_ref, got_ref[count:, half:]))
    ]
    gate_ref[...] = sums[0]
    send_ref[:, :half] = beside_ref[:, :half]
    send_ref[:, half : 2 * half] = got_ref[count:, :half]
    send_ref[:, 2 * half :] = sums[1]


def logit_body(gate_ref, got_ref, table_ref, vr_ref, or_ref, out_ref):
    both, count = out_ref.shape
    got = got_ref[:, got_ref.shape[1] - 128 :]
    near, far = gate_ref[...].astype(F32).T, got.astype(F32).T
    gates = table_ref[:count, :].T
    ids = lax.broadcasted_iota(jnp.int32, (both, count), 0)
    logit = jnp.zeros((both, count), F32)
    for side, (route_ref, first) in enumerate(((vr_ref, 0), (or_ref, both // 2))):
        for j in range(2):
            at = 2 * side + j
            grad = (near[at : at + 1] + near[4 + at : 5 + at]) + (
                far[at : at + 1] + far[4 + at : 5 + at]
            )
            gate = gates[at : at + 1]
            logit = jnp.where(
                ids == route_ref[j : j + 1, :] + first, grad * gate * (1.0 - gate), logit
            )
    out_ref[...] = logit


def chunk_sum_body(*refs):
    total = refs[0][...]
    for ref in refs[1:-1]:
        total += ref[...].astype(F32)
    refs[-1][...] = total.astype(BF16)


def final_sum_body(groups, *refs):
    total = refs[0][...]
    for ref in refs[1:-2]:
        total += ref[...].astype(F32)
    total = total / groups
    for side in range(2):
        refs[side - 2][0] = total[side]


def attention_back_body(probs_ref, q_ref, k_ref, mixed_ref, grad_ref, query_grad_ref, key_grad_ref):
    probs = probs_ref[...]
    prob_grad = dot_nt(grad_ref[...], mixed_ref[...])
    score_grad = probs * (prob_grad - jnp.sum(prob_grad * probs, axis=1, keepdims=True))
    scaled = score_grad / math.sqrt(q_ref.shape[1])
    query_grad_ref[...] = dot(scaled.astype(BF16), k_ref[...]).astype(BF16)
    key_grad_ref[...] = dot(scaled.T.astype(BF16), q_ref[...]).astype(BF16)


def on_device(
    tokens,
    queries,
    key_vectors,
    gate_logits,
    value_routes,
    output_routes,
    value_weight,
    output_weight,
    cotangent,
):
    count, features = tokens.shape
    size = queries.shape[1]
    experts = gate_logits.shape[1] // 2
    block = value_weight.shape[1]
    groups = lax.axis_size("dp")
    quads = groups // 4
    half = quads * block
    at = lax.axis_index("dp")
    me = lax.axis_index("expert")
    aligned = block % 128 == 0

    def over_dp(x, flip, what):
        with jax.named_scope(f"{what}_dp{flip}"):
            return lax.ppermute(x, "dp", [(i, i ^ flip) for i in range(groups)])

    def over_experts(x, flip, what):
        with jax.named_scope(f"{what}_expert{flip}"):
            return lax.ppermute(x, "expert", [(i, i ^ flip) for i in range(experts)])

    def side_by_side(arrays, axis):
        return arrays[0] if len(arrays) == 1 else jnp.concatenate(arrays, axis=axis)

    routing = (gate_logits.T, value_routes.T, output_routes.T)
    flips = ((2, 3), (1,), (0,))
    if aligned:
        own_banks, sent_rows, core_rows, own_rows = kernel_call(
            lambda *refs: pack_body(block, quads, flips, *refs),
            [((2, block, size), BF16)]
            + [((count, 2 * half * len(group) + 128), BF16) for group in flips],
            at[None],
            me[None],
            tokens,
            cotangent,
            value_weight,
            output_weight,
            *routing,
            scalars=2,
            where=pl.ANY,
            scratch=[pltpu.VMEM(x.shape, x.dtype) for x in routing]
            + [pltpu.SemaphoreType.DMA((5 + 8 * quads,))],
            vmem=60,
        )
    else:
        own_banks = jnp.concatenate([value_weight, output_weight], axis=0)
        (own_table,) = kernel_call(
            table_body, [((count, 128), BF16)], me[None], *routing, scalars=1
        )
        sent_rows, core_rows, own_rows = [
            jnp.concatenate(
                [
                    lax.dynamic_slice(x, (0, (at ^ (4 * k + flip)) * block), (count, block))
                    for flip in group
                    for x in (tokens, cotangent)
                    for k in range(quads)
                ]
                + [own_table],
                axis=1,
            )
            for group in flips
        ]
    first_round = [over_experts(own_banks, k, "banks") for k in range(1, experts)]
    other_banks = side_by_side([over_dp(own_banks, 4 * k, "banks") for k in range(1, quads)], 1)
    beside_rows = over_dp(sent_rows, 2, "rows")
    (other_banks,) = kernel_call(
        copy_body, [(other_banks.shape, BF16)], other_banks, flops=5000000000
    )
    other_banks, core_rows = lax.optimization_barrier(
        (other_banks, core_rows)
    )
    (far_rows,) = kernel_call(
        tail_body, [((count, 2 * half + 128), BF16)], beside_rows, flops=1000000000
    )
    banks = [own_banks, other_banks]
    for k in range(1, experts):
        banks += [first_round[k - 1], over_experts(other_banks, k, "other_banks")]
    rows = [
        own_rows,
        beside_rows,
        over_dp(core_rows, 1, "rows"),
        over_dp(far_rows, 1, "far_rows"),
    ]
    (table,) = kernel_call(
        lambda *refs: quad_table_body(experts, *refs), [((4 * count, 128), F32)], *rows
    )
    probs, weights = kernel_call(
        probs_body,
        [((count, count), F32), ((count, count), BF16)],
        queries,
        key_vectors,
    )

    turned_bank = [
        kernel_call(
            lambda *refs: turn_bank_body(size, *refs),
            [((experts * size, banks[chunk].shape[1]), BF16)],
            *banks[chunk::2],
            flops=flops,
        )[0]
        for chunk, flops in enumerate((0, 4000000000))
    ]
    (turned,) = kernel_call(turn_body, [((2 * half, 4 * count), BF16)], *rows)

    product_flops = 2 * 4 * count * half * experts * size
    table, turned_bank = lax.optimization_barrier((table, turned_bank))
    keep, send = kernel_call(
        lambda *refs: partial_body(experts, 2, size, half, *refs),
        [((2 * count, 2 * size), F32), ((2 * count, 2 * size), BF16)],
        *rows,
        table,
        *banks,
        flops=2 * product_flops,
    )
    (slots,) = kernel_call(
        lambda *refs: slots_body(experts, 2, size, half, *refs),
        [((4 * count, 4 * size), BF16)],
        *rows,
        table,
        *banks,
        flops=2 * product_flops,
    )
    chip_sum, send = kernel_call(
        core_sum_body,
        [((2 * count, 2 * size), F32), ((2 * count + count // 2, 2 * size), BF16)],
        keep,
        over_dp(send, 1, "partials"),
        weights,
    )
    got_sum, turned, turned_bank, slots = lax.optimization_barrier(
        (over_dp(send, 2, "partials"), turned, turned_bank, slots)
    )
    mixed_value, hidden_grad, head_rows = kernel_call(
        middle_body,
        [((count, size), BF16), ((count, size), BF16), ((2 * count, 2 * size), BF16)],
        chip_sum,
        got_sum,
        weights,
    )

    shapes = []
    for k in range(experts):
        kind = F32 if k == 0 else BF16
        shapes += [((2, block, size), kind), ((2, half - block, size), kind)]
    *grads, own_back, beside_back, core_back = kernel_call(
        lambda *refs: weight_grad_body(experts, 2, size, *refs),
        shapes + [((n * count, half + 128), BF16) for n in (1, 1, 2)],
        turned,
        *turned_bank,
        table,
        slots,
        head_rows,
        over_dp(head_rows, 1, "head_rows"),
        flops=3 * product_flops,
    )
    def over_all_experts(chunk):
        return [grads[chunk]] + [
            over_experts(grads[2 * k + chunk], k, "grads") for k in range(1, experts)
        ]

    far_chunk = over_all_experts(1)
    got_back = over_dp(core_back, 1, "token_back")
    gate_sums, beside_back = kernel_call(
        merge_body,
        [((count, 128), BF16), ((count, 2 * half + 128), BF16)],
        own_back,
        beside_back,
        got_back,
    )
    back = [own_back, got_back, over_dp(beside_back, 2, "token_back")]

    (others,) = kernel_call(
        chunk_sum_body, [((2, half - block, size), BF16)], *far_chunk, flops=1000000000
    )
    sums = over_all_experts(0) + [
        over_dp(others[:, (k - 1) * block : k * block], 4 * k, "grads") for k in range(1, quads)
    ]

    if aligned:
        (token_grad,) = kernel_call(
            lambda *refs: unpack_body(block, quads, *refs),
            [((count, features), BF16)],
            at[None],
            *back,
            scalars=1,
        )
    else:
        parts = jnp.concatenate(
            [back[0][:, :half], back[1][:count, :half], back[2][:, : 2 * half]], axis=1
        )
        token_grad = jnp.concatenate(
            [
                lax.dynamic_slice(
                    parts,
                    (0, (((at ^ b) & 3) * quads + ((at ^ b) >> 2)) * block),
                    (count, block),
                )
                for b in range(groups)
            ],
            axis=1,
        )

    (logit_grad,) = kernel_call(
        logit_body,
        [((2 * experts, count), F32)],
        gate_sums,
        back[2],
        table,
        value_routes.T,
        output_routes.T,
    )
    token_grad, logit_grad, sums = lax.optimization_barrier((token_grad, logit_grad, sums))
    value_weight_grad, output_weight_grad = kernel_call(
        lambda *refs: final_sum_body(groups, *refs), [((1, block, size), F32)] * 2, *sums
    )

    query_grad, key_grad = kernel_call(
        attention_back_body,
        [((count, size), BF16), ((count, size), BF16)],
        probs,
        queries,
        key_vectors,
        mixed_value,
        hidden_grad,
    )
    return (token_grad, query_grad, key_grad, logit_grad.T, value_weight_grad, output_weight_grad)


def solution(mesh):
    rows, banks = P(("dp", "expert"), None), P("expert", "dp", None)
    return jax.shard_map(
        on_device,
        mesh=mesh,
        in_specs=(rows,) * 6 + (banks, banks, rows),
        out_specs=(rows,) * 4 + (banks, banks),
        check_vma=False,
    )
```

```python
import math

import jax
import jax.numpy as jnp
from jax import lax
from jax.experimental import pallas as pl
from jax.experimental.pallas import tpu as pltpu
from jax.sharding import PartitionSpec as P

F32, BF16 = jnp.float32, jnp.bfloat16

def kernel_call(body, outs, *args, scalars=0, flops=0, moved=None, where=pltpu.VMEM, scratch=(), vmem=24):
    moved = moved or sum(x.size * x.dtype.itemsize for x in args) + sum(
        math.prod(s) * jnp.dtype(t).itemsize for s, t in outs
    )
    return pl.pallas_call(
        body,
        out_shape=[jax.ShapeDtypeStruct(s, t) for s, t in outs],
        in_specs=[pl.BlockSpec(memory_space=pltpu.SMEM)] * scalars
        + [pl.BlockSpec(memory_space=where)] * (len(args) - scalars),
        out_specs=[pl.BlockSpec(memory_space=pltpu.VMEM)] * len(outs),
        cost_estimate=pl.CostEstimate(flops=flops, bytes_accessed=moved, transcendentals=0),
        scratch_shapes=list(scratch),
        compiler_params=pltpu.CompilerParams(vmem_limit_bytes=vmem * 2**20),
    )(*args)


def dot(left, right):
    return jnp.dot(left, right, preferred_element_type=F32)


def dot_nt(left, right):
    return lax.dot_general(left, right, (((1,), (1,)), ((), ())), preferred_element_type=F32)


def probs_body(q_ref, k_ref, probs_ref, weights_ref):
    length = q_ref.shape[0]
    scores = dot_nt(q_ref[...], k_ref[...]) / math.sqrt(q_ref.shape[1])
    row_ids = lax.broadcasted_iota(jnp.int32, (length, length), 0)
    col_ids = lax.broadcasted_iota(jnp.int32, (length, length), 1)
    scores = jnp.where(row_ids >= col_ids, scores, -1e30)
    exponent = jnp.exp(scores - jnp.max(scores, axis=1, keepdims=True))
    probs = exponent / jnp.sum(exponent, axis=1, keepdims=True)
    probs_ref[...] = probs
    weights_ref[...] = probs.astype(BF16)


def token_table(me, logits, route_v, route_o):
    both, rows = logits.shape
    gates = jax.nn.sigmoid(logits)
    ids = lax.broadcasted_iota(jnp.int32, (both, rows), 0)
    dense = jnp.zeros((both, rows), F32)
    for routes, first in ((route_v, 0), (route_o, both // 2)):
        for j in range(2):
            route = routes[j : j + 1]
            gate = jnp.sum(jnp.where(ids == route + first, gates, 0.0), axis=0, keepdims=True)
            dense = jnp.where(ids == (route ^ me) + first, gate, dense)
    high = dense.astype(BF16).astype(F32)
    routes = [(routes ^ me).astype(F32) for routes in (route_v, route_o)]
    table = jnp.concatenate([high, dense - high] + routes, axis=0)
    return jnp.concatenate([table, jnp.zeros((128 - table.shape[0], rows), F32)], axis=0).T


def quad_table_body(experts, *refs):
    out_ref = refs[-1]
    both = 2 * experts
    for i, ref in enumerate(refs[:-1]):
        rows = ref.shape[0]
        table = ref[:, ref.shape[1] - 128 :].astype(F32)
        out_ref[i * rows : (i + 1) * rows, :] = jnp.concatenate(
            [table[:, :both] + table[:, both : 2 * both], table[:, both:]], axis=1
        )


def pack_body(block, quads, groups, at_ref, me_ref, tokens_ref, cotangent_ref, value_ref, output_ref, *refs):
    small_refs, bank_ref, out_refs, held_refs, sems = refs[:3], refs[3], refs[4:7], refs[7:10], refs[10]
    small = [
        pltpu.make_async_copy(ref, held, sems.at[i])
        for i, (ref, held) in enumerate(zip(small_refs, held_refs))
    ]
    copies = [
        pltpu.make_async_copy(ref.at[0], bank_ref.at[i], sems.at[3 + i])
        for i, ref in enumerate((value_ref, output_ref))
    ]
    for group, out_ref in zip(groups, out_refs):
        to = 0
        for flip in group:
            for ref in (tokens_ref, cotangent_ref):
                for k in range(quads):
                    start = pl.multiple_of((at_ref[0] ^ (4 * k + flip)) * block, block)
                    copies.append(
                        pltpu.make_async_copy(
                            ref.at[:, pl.ds(start, block)],
                            out_ref.at[:, to : to + block],
                            sems.at[3 + len(copies)],
                        )
                    )
                    to += block
    for copy in small + copies:
        copy.start()
    for copy in small:
        copy.wait()
    table = token_table(me_ref[0], *[held[...] for held in held_refs]).astype(BF16)
    for out_ref in out_refs:
        out_ref[:, out_ref.shape[1] - 128 :] = table
    for copy in copies:
        copy.wait()


def table_body(me_ref, logits_ref, vr_ref, or_ref, out_ref):
    out_ref[...] = token_table(me_ref[0], logits_ref[...], vr_ref[...], or_ref[...]).astype(BF16)


def unpack_body(block, quads, at_ref, own_ref, core_ref, beside_ref, out_ref):
    half = quads * block
    for flip, (ref, first) in enumerate(
        ((own_ref, 0), (core_ref, 0), (beside_ref, 0), (beside_ref, half))
    ):
        for k in range(quads):
            start = pl.multiple_of((at_ref[0] ^ (4 * k + flip)) * block, block)
            out_ref[:, pl.ds(start, block)] = ref[
                : out_ref.shape[0], first + k * block : first + (k + 1) * block
            ]


def turn_body(*refs):
    out_ref = refs[-1]
    for i, ref in enumerate(refs[:-1]):
        rows = ref.shape[0]
        out_ref[:, i * rows : (i + 1) * rows] = ref[:, : out_ref.shape[0]].T


def copy_body(in_ref, out_ref):
    out_ref[...] = in_ref[...]


def tail_body(in_ref, out_ref):
    out_ref[...] = in_ref[:, in_ref.shape[1] - out_ref.shape[1] :]


def turn_bank_body(size, *refs):
    for e, ref in enumerate(refs[:-1]):
        refs[-1][e * size : (e + 1) * size, :] = ref[0].T


def bank(refs, side):
    return jnp.concatenate([ref[side] for ref in refs], axis=0)


def bank_pair(refs, chunks, side, i):
    return jnp.concatenate(
        [bank(refs[e * chunks : (e + 1) * chunks], side) for e in (i, i + 1)], axis=1
    )


def expert_products(experts, chunks, half, side, row_refs, weights):
    left = jnp.concatenate([r[:, side * half : (side + 1) * half] for r in row_refs], axis=0)
    for i in range(0, experts, 2):
        product = dot(left, bank_pair(weights, chunks, side, i))
        size = product.shape[1] // 2
        yield i, product[:, :size]
        yield i + 1, product[:, size:]


def partial_body(experts, chunks, size, half, *refs):
    row_refs, table_ref, weights = refs[:4], refs[4], refs[5 : 5 + experts * chunks]
    keep_ref, send_ref = refs[-2:]
    count = row_refs[0].shape[0]
    for side in range(2):
        mixed = jnp.zeros((4 * count, size), F32)
        for e, product in expert_products(experts, chunks, half, side, row_refs, weights):
            at = side * experts + e
            mixed += table_ref[:, at : at + 1] * product
        lanes = slice(side * size, (side + 1) * size)
        keep_ref[:, lanes] = mixed[: 2 * count]
        send_ref[:, lanes] = mixed[2 * count :].astype(BF16)


def slots_body(experts, chunks, size, half, *refs):
    row_refs, table_ref, weights = refs[:4], refs[4], refs[5 : 5 + experts * chunks]
    slots_ref = refs[-1]
    count = row_refs[0].shape[0]
    for side in range(2):
        route = 4 * experts + 2 * side
        routes = [table_ref[:, route + j : route + j + 1] for j in range(2)]
        slots = [jnp.zeros((4 * count, size), F32) for _ in range(2)]
        for e, product in expert_products(experts, chunks, half, side, row_refs, weights):
            for j in range(2):
                slots[j] = jnp.where(routes[j] == float(e), product, slots[j])
        for j in range(2):
            slots_ref[:, (2 * side + j) * size : (2 * side + j + 1) * size] = slots[j].astype(BF16)


def core_sum_body(keep_ref, got_ref, sum_ref, send_ref):
    total = keep_ref[...] + got_ref[...].astype(F32)
    sum_ref[...] = total
    send_ref[...] = total.astype(BF16)


def middle_body(sum_ref, got_ref, weights_ref, far_weights_ref, mixed_ref, grad_ref, rows_ref):
    count, size = mixed_ref.shape
    for i, weights in enumerate((weights_ref[...], far_weights_ref[...])):
        total = sum_ref[i * count : (i + 1) * count, :] + got_ref[
            (1 - i) * count : (2 - i) * count, :
        ].astype(F32)
        total = total.astype(BF16)
        if i == 0:
            mixed_ref[...], grad_ref[...] = total[:, :size], total[:, size:]
        rows_ref[i * count : (i + 1) * count, :size] = dot(weights, total[:, :size]).astype(BF16)
        rows_ref[i * count : (i + 1) * count, size:] = lax.dot_general(
            weights, total[:, size:], (((0,), (0,)), ((), ())), preferred_element_type=F32
        ).astype(BF16)


def two_parts(columns):
    rows = columns[0].shape[0]
    lane = lax.broadcasted_iota(jnp.int32, (rows, 128), 1)
    block = jnp.zeros((rows, 128), F32)
    for j, column in enumerate(columns):
        high = column.astype(BF16).astype(F32)
        block = jnp.where(lane == j, high, block)
        block = jnp.where(lane == 4 + j, column - high, block)
    return block.astype(BF16)


def whole_columns(block):
    block = block.astype(F32)
    return [block[:, j : j + 1] + block[:, 4 + j : 5 + j] for j in range(4)]


def gated_rows(experts, side, table_ref, rows):
    first = side * experts
    return [
        (table_ref[:, e : e + 1] * rows).astype(BF16) for e in range(first, first + experts)
    ]


def weight_grad_body(experts, chunks, size, turned_ref, *refs):
    bank_refs, (table_ref, slots_ref), refs = refs[:2], refs[2:4], refs[4:]
    row_refs, out_refs, back_refs = refs[:2], refs[2:-3], refs[-3:]
    half, count = turned_ref.shape[0] // 2, row_refs[0].shape[0] // 2
    gate_grads = []
    for side, at in ((0, 1), (1, 0)):
        rows = jnp.concatenate([r[:, at * size : (at + 1) * size] for r in row_refs], axis=0)
        rows = rows.astype(F32)
        gated = gated_rows(experts, side, table_ref, rows)
        left = turned_ref[side * half : (side + 1) * half, :]
        for i in range(0, experts, 2):
            product = dot(left, jnp.concatenate(gated[i : i + 2], axis=1))
            for p in range(2):
                start = 0
                for out_ref in out_refs[(i + p) * chunks : (i + p + 1) * chunks]:
                    stop = start + out_ref.shape[1]
                    out_ref[side] = product[start:stop, p * size : (p + 1) * size].astype(
                        out_ref.dtype
                    )
                    start = stop
        if side == 0:
            bank_rows = jnp.concatenate([ref[...] for ref in bank_refs], axis=1)
            back = dot(jnp.concatenate(gated, axis=1), bank_rows).astype(BF16)
        for j in range(2):
            slot = slots_ref[:, (2 * side + j) * size : (2 * side + j + 1) * size].astype(F32)
            gate_grads.append(jnp.sum(rows * slot, axis=1, keepdims=True))
    gate_block = two_parts(gate_grads)
    for i, back_ref in enumerate(back_refs):
        start, stop = (i * count, (i + 1) * count) if i < 2 else (2 * count, 4 * count)
        back_ref[:, :half] = back[start:stop]
        back_ref[:, half:] = gate_block[start:stop]


def merge_body(own_ref, beside_ref, got_ref, gate_ref, send_ref):
    count, half = beside_ref.shape[0], beside_ref.shape[1] - 128
    sums = [
        two_parts(
            [
                near + far
                for near, far in zip(whole_columns(ref[:, half:]), whole_columns(got))
            ]
        )
        for ref, got in ((own_ref, got_ref[:count, half:]), (beside_ref, got_ref[count:, half:]))
    ]
    gate_ref[...] = sums[0]
    send_ref[:, :half] = beside_ref[:, :half]
    send_ref[:, half : 2 * half] = got_ref[count:, :half]
    send_ref[:, 2 * half :] = sums[1]


def logit_body(gate_ref, got_ref, table_ref, vr_ref, or_ref, out_ref):
    both, count = out_ref.shape
    got = got_ref[:, got_ref.shape[1] - 128 :]
    near, far = gate_ref[...].astype(F32).T, got.astype(F32).T
    table = table_ref[:count, :].T
    ids = lax.broadcasted_iota(jnp.int32, (both, count), 0)
    logit = jnp.zeros((both, count), F32)
    for side, route_ref in enumerate((vr_ref, or_ref)):
        first = side * (both // 2)
        for j in range(2):
            at = 2 * side + j
            grad = (near[at : at + 1] + near[4 + at : 5 + at]) + (
                far[at : at + 1] + far[4 + at : 5 + at]
            )
            here = ids.astype(F32) == table[2 * both + at : 2 * both + at + 1] + float(first)
            gate = jnp.sum(jnp.where(here, table[:both], 0.0), axis=0, keepdims=True)
            logit = jnp.where(
                ids == route_ref[j : j + 1, :] + first, grad * gate * (1.0 - gate), logit
            )
    out_ref[...] = logit


def chunk_sum_body(*refs):
    total = refs[0][...]
    for ref in refs[1:-1]:
        total += ref[...].astype(F32)
    refs[-1][...] = total.astype(BF16)


def final_sum_body(groups, *refs):
    total = refs[0][...]
    for ref in refs[1:-2]:
        total += ref[...].astype(F32)
    total = total / groups
    for side in range(2):
        refs[side - 2][0] = total[side]


def attention_back_body(probs_ref, q_ref, k_ref, mixed_ref, grad_ref, query_grad_ref, key_grad_ref):
    probs = probs_ref[...]
    prob_grad = dot_nt(grad_ref[...], mixed_ref[...])
    score_grad = probs * (prob_grad - jnp.sum(prob_grad * probs, axis=1, keepdims=True))
    scaled = score_grad / math.sqrt(q_ref.shape[1])
    query_grad_ref[...] = dot(scaled.astype(BF16), k_ref[...]).astype(BF16)
    key_grad_ref[...] = dot(scaled.T.astype(BF16), q_ref[...]).astype(BF16)


def on_device(
    tokens,
    queries,
    key_vectors,
    gate_logits,
    value_routes,
    output_routes,
    value_weight,
    output_weight,
    cotangent,
):
    count, features = tokens.shape
    size = queries.shape[1]
    experts = gate_logits.shape[1] // 2
    block = value_weight.shape[1]
    groups = lax.axis_size("dp")
    quads = groups // 4
    half = quads * block
    at = lax.axis_index("dp")
    me = lax.axis_index("expert")
    aligned = block % 128 == 0

    def over_dp(x, flip, what):
        with jax.named_scope(f"{what}_dp{flip}"):
            return lax.ppermute(x, "dp", [(i, i ^ flip) for i in range(groups)])

    def over_experts(x, flip, what):
        with jax.named_scope(f"{what}_expert{flip}"):
            return lax.ppermute(x, "expert", [(i, i ^ flip) for i in range(experts)])

    def side_by_side(arrays, axis):
        return arrays[0] if len(arrays) == 1 else jnp.concatenate(arrays, axis=axis)

    routing = (gate_logits.T, value_routes.T, output_routes.T)
    flips = ((2, 3), (1,), (0,))
    if aligned:
        own_banks, sent_rows, core_rows, own_rows = kernel_call(
            lambda *refs: pack_body(block, quads, flips, *refs),
            [((2, block, size), BF16)]
            + [((count, 2 * half * len(group) + 128), BF16) for group in flips],
            at[None],
            me[None],
            tokens,
            cotangent,
            value_weight,
            output_weight,
            *routing,
            scalars=2,
            where=pl.ANY,
            scratch=[pltpu.VMEM(x.shape, x.dtype) for x in routing]
            + [pltpu.SemaphoreType.DMA((5 + 8 * quads,))],
            vmem=60,
        )
    else:
        own_banks = jnp.concatenate([value_weight, output_weight], axis=0)
        (own_table,) = kernel_call(
            table_body, [((count, 128), BF16)], me[None], *routing, scalars=1
        )
        sent_rows, core_rows, own_rows = [
            jnp.concatenate(
                [
                    lax.dynamic_slice(x, (0, (at ^ (4 * k + flip)) * block), (count, block))
                    for flip in group
                    for x in (tokens, cotangent)
                    for k in range(quads)
                ]
                + [own_table],
                axis=1,
            )
            for group in flips
        ]
    first_round = [over_experts(own_banks, k, "banks") for k in range(1, experts)]
    other_banks = side_by_side([over_dp(own_banks, 4 * k, "banks") for k in range(1, quads)], 1)
    beside_rows = over_dp(sent_rows, 2, "rows")
    (other_banks,) = kernel_call(
        copy_body, [(other_banks.shape, BF16)], other_banks, flops=5000000000
    )
    other_banks, core_rows = lax.optimization_barrier(
        (other_banks, core_rows)
    )
    (far_rows,) = kernel_call(
        tail_body, [((count, 2 * half + 128), BF16)], beside_rows, flops=1000000000
    )
    banks = [own_banks, other_banks]
    for k in range(1, experts):
        banks += [first_round[k - 1], over_experts(other_banks, k, "other_banks")]
    rows = [
        own_rows,
        beside_rows,
        over_dp(core_rows, 1, "rows"),
        over_dp(far_rows, 1, "far_rows"),
    ]
    probs, weights = kernel_call(
        probs_body,
        [((count, count), F32), ((count, count), BF16)],
        queries,
        key_vectors,
    )
    far_weights = over_dp(weights, 2, "weights")
    (table,) = kernel_call(
        lambda *refs: quad_table_body(experts, *refs[:4], refs[-1]),
        [((4 * count, 128), F32)],
        *rows,
        far_weights,
    )

    turned_bank = [
        kernel_call(
            lambda *refs: turn_bank_body(size, *refs),
            [((experts * size, banks[chunk].shape[1]), BF16)],
            *banks[chunk::2],
            flops=flops,
        )[0]
        for chunk, flops in enumerate((0, 4000000000))
    ]
    (turned,) = kernel_call(turn_body, [((2 * half, 4 * count), BF16)], *rows)

    product_flops = 2 * 4 * count * half * experts * size
    table, turned_bank = lax.optimization_barrier((table, turned_bank))
    keep, send = kernel_call(
        lambda *refs: partial_body(experts, 2, size, half, *refs),
        [((2 * count, 2 * size), F32), ((2 * count, 2 * size), BF16)],
        *rows,
        table,
        *banks,
        flops=2 * product_flops,
    )
    (slots,) = kernel_call(
        lambda *refs: slots_body(experts, 2, size, half, *refs),
        [((4 * count, 4 * size), BF16)],
        *rows,
        table,
        *banks,
        flops=2 * product_flops,
    )
    chip_sum, send = kernel_call(
        core_sum_body,
        [((2 * count, 2 * size), F32), ((2 * count, 2 * size), BF16)],
        keep,
        over_dp(send, 1, "partials"),
    )
    got_sum, turned, turned_bank, slots = lax.optimization_barrier(
        (over_dp(send, 2, "partials"), turned, turned_bank, slots)
    )
    mixed_value, hidden_grad, head_rows = kernel_call(
        middle_body,
        [((count, size), BF16), ((count, size), BF16), ((2 * count, 2 * size), BF16)],
        chip_sum,
        got_sum,
        weights,
        far_weights,
    )

    shapes = []
    for k in range(experts):
        kind = F32 if k == 0 else BF16
        shapes += [((2, block, size), kind), ((2, half - block, size), kind)]
    *grads, own_back, beside_back, core_back = kernel_call(
        lambda *refs: weight_grad_body(experts, 2, size, *refs),
        shapes + [((n * count, half + 128), BF16) for n in (1, 1, 2)],
        turned,
        *turned_bank,
        table,
        slots,
        head_rows,
        over_dp(head_rows, 1, "head_rows"),
        flops=3 * product_flops,
    )
    def over_all_experts(chunk):
        return [grads[chunk]] + [
            over_experts(grads[2 * k + chunk], k, "grads") for k in range(1, experts)
        ]

    far_chunk = over_all_experts(1)
    got_back = over_dp(core_back, 1, "token_back")
    gate_sums, beside_back = kernel_call(
        merge_body,
        [((count, 128), BF16), ((count, 2 * half + 128), BF16)],
        own_back,
        beside_back,
        got_back,
    )
    back = [own_back, got_back, over_dp(beside_back, 2, "token_back")]

    (others,) = kernel_call(
        chunk_sum_body, [((2, half - block, size), BF16)], *far_chunk, flops=1000000000
    )
    sums = over_all_experts(0) + [
        over_dp(others[:, (k - 1) * block : k * block], 4 * k, "grads") for k in range(1, quads)
    ]

    if aligned:
        (token_grad,) = kernel_call(
            lambda *refs: unpack_body(block, quads, *refs),
            [((count, features), BF16)],
            at[None],
            *back,
            scalars=1,
        )
    else:
        parts = jnp.concatenate(
            [back[0][:, :half], back[1][:count, :half], back[2][:, : 2 * half]], axis=1
        )
        token_grad = jnp.concatenate(
            [
                lax.dynamic_slice(
                    parts,
                    (0, (((at ^ b) & 3) * quads + ((at ^ b) >> 2)) * block),
                    (count, block),
                )
                for b in range(groups)
            ],
            axis=1,
        )

    (logit_grad,) = kernel_call(
        logit_body,
        [((2 * experts, count), F32)],
        gate_sums,
        back[2],
        table,
        value_routes.T,
        output_routes.T,
    )
    token_grad, logit_grad, sums = lax.optimization_barrier((token_grad, logit_grad, sums))
    value_weight_grad, output_weight_grad = kernel_call(
        lambda *refs: final_sum_body(groups, *refs), [((1, block, size), F32)] * 2, *sums
    )

    query_grad, key_grad = kernel_call(
        attention_back_body,
        [((count, size), BF16), ((count, size), BF16)],
        probs,
        queries,
        key_vectors,
        mixed_value,
        hidden_grad,
    )
    return (token_grad, query_grad, key_grad, logit_grad.T, value_weight_grad, output_weight_grad)


def solution(mesh):
    rows, banks = P(("dp", "expert"), None), P("expert", "dp", None)
    return jax.shard_map(
        on_device,
        mesh=mesh,
        in_specs=(rows,) * 6 + (banks, banks, rows),
        out_specs=(rows,) * 4 + (banks, banks),
        check_vma=False,
    )
```

```python
import math

import jax
import jax.numpy as jnp
from jax import lax
from jax.experimental import pallas as pl
from jax.experimental.pallas import tpu as pltpu
from jax.sharding import PartitionSpec as P

F32, BF16 = jnp.float32, jnp.bfloat16

def kernel_call(body, outs, *args, scalars=0, flops=0, moved=None, where=pltpu.VMEM, scratch=(), vmem=24):
    moved = moved or sum(x.size * x.dtype.itemsize for x in args) + sum(
        math.prod(s) * jnp.dtype(t).itemsize for s, t in outs
    )
    return pl.pallas_call(
        body,
        out_shape=[jax.ShapeDtypeStruct(s, t) for s, t in outs],
        in_specs=[pl.BlockSpec(memory_space=pltpu.SMEM)] * scalars
        + [pl.BlockSpec(memory_space=where)] * (len(args) - scalars),
        out_specs=[pl.BlockSpec(memory_space=pltpu.VMEM)] * len(outs),
        cost_estimate=pl.CostEstimate(flops=flops, bytes_accessed=moved, transcendentals=0),
        scratch_shapes=list(scratch),
        compiler_params=pltpu.CompilerParams(vmem_limit_bytes=vmem * 2**20),
    )(*args)


def dot(left, right):
    return jnp.dot(left, right, preferred_element_type=F32)


def dot_nt(left, right):
    return lax.dot_general(left, right, (((1,), (1,)), ((), ())), preferred_element_type=F32)


def probs_body(q_ref, k_ref, probs_ref, weights_ref):
    length = q_ref.shape[0]
    scores = dot_nt(q_ref[...], k_ref[...]) / math.sqrt(q_ref.shape[1])
    row_ids = lax.broadcasted_iota(jnp.int32, (length, length), 0)
    col_ids = lax.broadcasted_iota(jnp.int32, (length, length), 1)
    scores = jnp.where(row_ids >= col_ids, scores, -1e30)
    exponent = jnp.exp(scores - jnp.max(scores, axis=1, keepdims=True))
    probs = exponent / jnp.sum(exponent, axis=1, keepdims=True)
    probs_ref[...] = probs
    weights_ref[...] = probs.astype(BF16)


def token_table(me, logits, route_v, route_o):
    both, rows = logits.shape
    gates = jax.nn.sigmoid(logits)
    ids = lax.broadcasted_iota(jnp.int32, (both, rows), 0)
    dense = jnp.zeros((both, rows), F32)
    for routes, first in ((route_v, 0), (route_o, both // 2)):
        for j in range(2):
            route = routes[j : j + 1]
            gate = jnp.sum(jnp.where(ids == route + first, gates, 0.0), axis=0, keepdims=True)
            dense = jnp.where(ids == (route ^ me) + first, gate, dense)
    high = dense.astype(BF16).astype(F32)
    routes = [(routes ^ me).astype(F32) for routes in (route_v, route_o)]
    table = jnp.concatenate([high, dense - high] + routes, axis=0)
    return jnp.concatenate([table, jnp.zeros((128 - table.shape[0], rows), F32)], axis=0).T


def quad_table_body(experts, *refs):
    out_ref = refs[-1]
    both = 2 * experts
    for i, ref in enumerate(refs[:-1]):
        rows = ref.shape[0]
        table = ref[:, ref.shape[1] - 128 :].astype(F32)
        out_ref[i * rows : (i + 1) * rows, :] = jnp.concatenate(
            [table[:, :both] + table[:, both : 2 * both], table[:, both:]], axis=1
        )


def pack_body(block, quads, groups, bank_count, at_ref, me_ref, tokens_ref, cotangent_ref, *refs):
    bank_refs, refs = refs[:bank_count], refs[bank_count:]
    small_refs, held_refs, sems = refs[:3], refs[-4:-1], refs[-1]
    out_refs = refs[-4 - len(groups) : -4]
    small = [
        pltpu.make_async_copy(ref, held, sems.at[i])
        for i, (ref, held) in enumerate(zip(small_refs, held_refs))
    ]
    copies = [
        pltpu.make_async_copy(ref.at[0], refs[3].at[i], sems.at[3 + i])
        for i, ref in enumerate(bank_refs)
    ]
    for group, out_ref in zip(groups, out_refs):
        to = 0
        for flip in group:
            for ref in (tokens_ref, cotangent_ref):
                for k in range(quads):
                    start = pl.multiple_of((at_ref[0] ^ (4 * k + flip)) * block, block)
                    copies.append(
                        pltpu.make_async_copy(
                            ref.at[:, pl.ds(start, block)],
                            out_ref.at[:, to : to + block],
                            sems.at[3 + len(copies)],
                        )
                    )
                    to += block
    for copy in small + copies:
        copy.start()
    for copy in small:
        copy.wait()
    table = token_table(me_ref[0], *[held[...] for held in held_refs]).astype(BF16)
    for out_ref in out_refs:
        out_ref[:, out_ref.shape[1] - 128 :] = table
    for copy in copies:
        copy.wait()


def table_body(me_ref, logits_ref, vr_ref, or_ref, out_ref):
    out_ref[...] = token_table(me_ref[0], logits_ref[...], vr_ref[...], or_ref[...]).astype(BF16)


def unpack_body(block, quads, at_ref, own_ref, core_ref, beside_ref, out_ref):
    half = quads * block
    for flip, (ref, first) in enumerate(
        ((own_ref, 0), (core_ref, 0), (beside_ref, 0), (beside_ref, half))
    ):
        for k in range(quads):
            start = pl.multiple_of((at_ref[0] ^ (4 * k + flip)) * block, block)
            out_ref[:, pl.ds(start, block)] = ref[
                : out_ref.shape[0], first + k * block : first + (k + 1) * block
            ]


def turn_body(*refs):
    out_ref = refs[-1]
    for i, ref in enumerate(refs[:-1]):
        rows = ref.shape[0]
        out_ref[:, i * rows : (i + 1) * rows] = ref[:, : out_ref.shape[0]].T


def copy_body(in_ref, out_ref):
    out_ref[...] = in_ref[...]


def tail_body(in_ref, out_ref):
    out_ref[...] = in_ref[:, in_ref.shape[1] - out_ref.shape[1] :]


def turn_bank_body(size, *refs):
    for e, ref in enumerate(refs[:-1]):
        refs[-1][e * size : (e + 1) * size, :] = ref[0].T


def bank(refs, side):
    return jnp.concatenate([ref[side] for ref in refs], axis=0)


def bank_pair(refs, chunks, side, i):
    return jnp.concatenate(
        [bank(refs[e * chunks : (e + 1) * chunks], side) for e in (i, i + 1)], axis=1
    )


def expert_products(experts, chunks, half, side, row_refs, weights):
    left = jnp.concatenate([r[:, side * half : (side + 1) * half] for r in row_refs], axis=0)
    for i in range(0, experts, 2):
        product = dot(left, bank_pair(weights, chunks, side, i))
        size = product.shape[1] // 2
        yield i, product[:, :size]
        yield i + 1, product[:, size:]


def partial_body(experts, chunks, size, half, *refs):
    row_refs, table_ref, weights = refs[:4], refs[4], refs[5 : 5 + experts * chunks]
    keep_ref, send_ref = refs[-2:]
    count = row_refs[0].shape[0]
    for side in range(2):
        mixed = jnp.zeros((4 * count, size), F32)
        for e, product in expert_products(experts, chunks, half, side, row_refs, weights):
            at = side * experts + e
            mixed += table_ref[:, at : at + 1] * product
        lanes = slice(side * size, (side + 1) * size)
        keep_ref[:, lanes] = mixed[: 2 * count]
        send_ref[:, lanes] = mixed[2 * count :].astype(BF16)


def slots_body(experts, chunks, size, half, *refs):
    row_refs, table_ref, weights = refs[:4], refs[4], refs[5 : 5 + experts * chunks]
    slots_ref = refs[-1]
    count = row_refs[0].shape[0]
    for side in range(2):
        route = 4 * experts + 2 * side
        routes = [table_ref[:, route + j : route + j + 1] for j in range(2)]
        slots = [jnp.zeros((4 * count, size), F32) for _ in range(2)]
        for e, product in expert_products(experts, chunks, half, side, row_refs, weights):
            for j in range(2):
                slots[j] = jnp.where(routes[j] == float(e), product, slots[j])
        for j in range(2):
            slots_ref[:, (2 * side + j) * size : (2 * side + j + 1) * size] = slots[j].astype(BF16)


def core_sum_body(keep_ref, got_ref, sum_ref, send_ref):
    total = keep_ref[...] + got_ref[...].astype(F32)
    sum_ref[...] = total
    send_ref[...] = total.astype(BF16)


def middle_body(sum_ref, got_ref, weights_ref, far_weights_ref, mixed_ref, grad_ref, rows_ref):
    count, size = mixed_ref.shape
    for i, weights in enumerate((weights_ref[...], far_weights_ref[...])):
        total = sum_ref[i * count : (i + 1) * count, :] + got_ref[
            (1 - i) * count : (2 - i) * count, :
        ].astype(F32)
        total = total.astype(BF16)
        if i == 0:
            mixed_ref[...], grad_ref[...] = total[:, :size], total[:, size:]
        rows_ref[i * count : (i + 1) * count, :size] = dot(weights, total[:, :size]).astype(BF16)
        rows_ref[i * count : (i + 1) * count, size:] = lax.dot_general(
            weights, total[:, size:], (((0,), (0,)), ((), ())), preferred_element_type=F32
        ).astype(BF16)


def two_parts(columns):
    rows = columns[0].shape[0]
    lane = lax.broadcasted_iota(jnp.int32, (rows, 128), 1)
    block = jnp.zeros((rows, 128), F32)
    for j, column in enumerate(columns):
        high = column.astype(BF16).astype(F32)
        block = jnp.where(lane == j, high, block)
        block = jnp.where(lane == 4 + j, column - high, block)
    return block.astype(BF16)


def whole_columns(block):
    block = block.astype(F32)
    return [block[:, j : j + 1] + block[:, 4 + j : 5 + j] for j in range(4)]


def gated_rows(experts, side, table_ref, rows):
    first = side * experts
    return [
        (table_ref[:, e : e + 1] * rows).astype(BF16) for e in range(first, first + experts)
    ]


def weight_grad_body(experts, chunks, size, turned_ref, *refs):
    bank_refs, (table_ref, slots_ref), refs = refs[:2], refs[2:4], refs[4:]
    row_refs, out_refs, back_refs = refs[:2], refs[2:-3], refs[-3:]
    half, count = turned_ref.shape[0] // 2, row_refs[0].shape[0] // 2
    gate_grads = []
    for side, at in ((0, 1), (1, 0)):
        rows = jnp.concatenate([r[:, at * size : (at + 1) * size] for r in row_refs], axis=0)
        rows = rows.astype(F32)
        gated = gated_rows(experts, side, table_ref, rows)
        left = turned_ref[side * half : (side + 1) * half, :]
        for i in range(0, experts, 2):
            product = dot(left, jnp.concatenate(gated[i : i + 2], axis=1))
            for p in range(2):
                start = 0
                for out_ref in out_refs[(i + p) * chunks : (i + p + 1) * chunks]:
                    stop = start + out_ref.shape[1]
                    out_ref[side] = product[start:stop, p * size : (p + 1) * size].astype(
                        out_ref.dtype
                    )
                    start = stop
        if side == 0:
            bank_rows = jnp.concatenate([ref[...] for ref in bank_refs], axis=1)
            back = dot(jnp.concatenate(gated, axis=1), bank_rows).astype(BF16)
        for j in range(2):
            slot = slots_ref[:, (2 * side + j) * size : (2 * side + j + 1) * size].astype(F32)
            gate_grads.append(jnp.sum(rows * slot, axis=1, keepdims=True))
    gate_block = two_parts(gate_grads)
    for i, back_ref in enumerate(back_refs):
        start, stop = (i * count, (i + 1) * count) if i < 2 else (2 * count, 4 * count)
        back_ref[:, :half] = back[start:stop]
        back_ref[:, half:] = gate_block[start:stop]


def merge_body(own_ref, beside_ref, got_ref, gate_ref, send_ref):
    count, half = beside_ref.shape[0], beside_ref.shape[1] - 128
    sums = [
        two_parts(
            [
                near + far
                for near, far in zip(whole_columns(ref[:, half:]), whole_columns(got))
            ]
        )
        for ref, got in ((own_ref, got_ref[:count, half:]), (beside_ref, got_ref[count:, half:]))
    ]
    gate_ref[...] = sums[0]
    send_ref[:, :half] = beside_ref[:, :half]
    send_ref[:, half : 2 * half] = got_ref[count:, :half]
    send_ref[:, 2 * half :] = sums[1]


def logit_body(gate_ref, got_ref, table_ref, vr_ref, or_ref, out_ref):
    both, count = out_ref.shape
    got = got_ref[:, got_ref.shape[1] - 128 :]
    near, far = gate_ref[...].astype(F32).T, got.astype(F32).T
    table = table_ref[:count, :].T
    ids = lax.broadcasted_iota(jnp.int32, (both, count), 0)
    logit = jnp.zeros((both, count), F32)
    for side, route_ref in enumerate((vr_ref, or_ref)):
        first = side * (both // 2)
        for j in range(2):
            at = 2 * side + j
            grad = (near[at : at + 1] + near[4 + at : 5 + at]) + (
                far[at : at + 1] + far[4 + at : 5 + at]
            )
            here = ids.astype(F32) == table[2 * both + at : 2 * both + at + 1] + float(first)
            gate = jnp.sum(jnp.where(here, table[:both], 0.0), axis=0, keepdims=True)
            logit = jnp.where(
                ids == route_ref[j : j + 1, :] + first, grad * gate * (1.0 - gate), logit
            )
    out_ref[...] = logit


def chunk_sum_body(*refs):
    total = refs[0][...]
    for ref in refs[1:-1]:
        total += ref[...].astype(F32)
    refs[-1][...] = total.astype(BF16)


def final_sum_body(groups, *refs):
    total = refs[0][...]
    for ref in refs[1:-2]:
        total += ref[...].astype(F32)
    total = total / groups
    for side in range(2):
        refs[side - 2][0] = total[side]


def attention_back_body(probs_ref, q_ref, k_ref, mixed_ref, grad_ref, query_grad_ref, key_grad_ref):
    probs = probs_ref[...]
    prob_grad = dot_nt(grad_ref[...], mixed_ref[...])
    score_grad = probs * (prob_grad - jnp.sum(prob_grad * probs, axis=1, keepdims=True))
    scaled = score_grad / math.sqrt(q_ref.shape[1])
    query_grad_ref[...] = dot(scaled.astype(BF16), k_ref[...]).astype(BF16)
    key_grad_ref[...] = dot(scaled.T.astype(BF16), q_ref[...]).astype(BF16)


def on_device(
    tokens,
    queries,
    key_vectors,
    gate_logits,
    value_routes,
    output_routes,
    value_weight,
    output_weight,
    cotangent,
):
    count, features = tokens.shape
    size = queries.shape[1]
    experts = gate_logits.shape[1] // 2
    block = value_weight.shape[1]
    groups = lax.axis_size("dp")
    quads = groups // 4
    half = quads * block
    at = lax.axis_index("dp")
    me = lax.axis_index("expert")
    aligned = block % 128 == 0

    def over_dp(x, flip, what):
        with jax.named_scope(f"{what}_dp{flip}"):
            return lax.ppermute(x, "dp", [(i, i ^ flip) for i in range(groups)])

    def over_experts(x, flip, what):
        with jax.named_scope(f"{what}_expert{flip}"):
            return lax.ppermute(x, "expert", [(i, i ^ flip) for i in range(experts)])

    def side_by_side(arrays, axis):
        return arrays[0] if len(arrays) == 1 else jnp.concatenate(arrays, axis=axis)

    routing = (gate_logits.T, value_routes.T, output_routes.T)
    flips = ((2, 3), (1,), (0,))
    if aligned:

        def pack(groups, *banks):
            return kernel_call(
                lambda *refs: pack_body(block, quads, groups, len(banks), *refs),
                [((2, block, size), BF16)] * (len(banks) // 2)
                + [((count, 2 * half * len(group) + 128), BF16) for group in groups],
                at[None],
                me[None],
                tokens,
                cotangent,
                *banks,
                *routing,
                scalars=2,
                where=pl.ANY,
                scratch=[pltpu.VMEM(x.shape, x.dtype) for x in routing]
                + [pltpu.SemaphoreType.DMA((5 + 8 * quads,))],
                vmem=60,
            )

        own_banks, sent_rows = pack(flips[:1], value_weight, output_weight)
        core_rows, own_rows = pack(flips[1:])
    else:
        own_banks = jnp.concatenate([value_weight, output_weight], axis=0)
        (own_table,) = kernel_call(
            table_body, [((count, 128), BF16)], me[None], *routing, scalars=1
        )
        sent_rows, core_rows, own_rows = [
            jnp.concatenate(
                [
                    lax.dynamic_slice(x, (0, (at ^ (4 * k + flip)) * block), (count, block))
                    for flip in group
                    for x in (tokens, cotangent)
                    for k in range(quads)
                ]
                + [own_table],
                axis=1,
            )
            for group in flips
        ]
    first_round = [over_experts(own_banks, k, "banks") for k in range(1, experts)]
    other_banks = side_by_side([over_dp(own_banks, 4 * k, "banks") for k in range(1, quads)], 1)
    beside_rows = over_dp(sent_rows, 2, "rows")
    (other_banks,) = kernel_call(
        copy_body, [(other_banks.shape, BF16)], other_banks, flops=5000000000
    )
    other_banks, core_rows = lax.optimization_barrier(
        (other_banks, core_rows)
    )
    (far_rows,) = kernel_call(
        tail_body, [((count, 2 * half + 128), BF16)], beside_rows, flops=1000000000
    )
    banks = [own_banks, other_banks]
    for k in range(1, experts):
        banks += [first_round[k - 1], over_experts(other_banks, k, "other_banks")]
    rows = [
        own_rows,
        beside_rows,
        over_dp(core_rows, 1, "rows"),
        over_dp(far_rows, 1, "far_rows"),
    ]
    probs, weights = kernel_call(
        probs_body,
        [((count, count), F32), ((count, count), BF16)],
        queries,
        key_vectors,
    )
    far_weights = over_dp(weights, 2, "weights")
    (table,) = kernel_call(
        lambda *refs: quad_table_body(experts, *refs[:4], refs[-1]),
        [((4 * count, 128), F32)],
        *rows,
        far_weights,
    )

    turned_bank = [
        kernel_call(
            lambda *refs: turn_bank_body(size, *refs),
            [((experts * size, banks[chunk].shape[1]), BF16)],
            *banks[chunk::2],
            flops=flops,
        )[0]
        for chunk, flops in enumerate((0, 4000000000))
    ]
    (turned,) = kernel_call(turn_body, [((2 * half, 4 * count), BF16)], *rows)

    product_flops = 2 * 4 * count * half * experts * size
    table, turned_bank = lax.optimization_barrier((table, turned_bank))
    keep, send = kernel_call(
        lambda *refs: partial_body(experts, 2, size, half, *refs),
        [((2 * count, 2 * size), F32), ((2 * count, 2 * size), BF16)],
        *rows,
        table,
        *banks,
        flops=2 * product_flops,
    )
    (slots,) = kernel_call(
        lambda *refs: slots_body(experts, 2, size, half, *refs),
        [((4 * count, 4 * size), BF16)],
        *rows,
        table,
        *banks,
        flops=2 * product_flops,
    )
    chip_sum, send = kernel_call(
        core_sum_body,
        [((2 * count, 2 * size), F32), ((2 * count, 2 * size), BF16)],
        keep,
        over_dp(send, 1, "partials"),
    )
    got_sum, turned, turned_bank, slots = lax.optimization_barrier(
        (over_dp(send, 2, "partials"), turned, turned_bank, slots)
    )
    mixed_value, hidden_grad, head_rows = kernel_call(
        middle_body,
        [((count, size), BF16), ((count, size), BF16), ((2 * count, 2 * size), BF16)],
        chip_sum,
        got_sum,
        weights,
        far_weights,
    )

    shapes = []
    for k in range(experts):
        kind = F32 if k == 0 else BF16
        shapes += [((2, block, size), kind), ((2, half - block, size), kind)]
    *grads, own_back, beside_back, core_back = kernel_call(
        lambda *refs: weight_grad_body(experts, 2, size, *refs),
        shapes + [((n * count, half + 128), BF16) for n in (1, 1, 2)],
        turned,
        *turned_bank,
        table,
        slots,
        head_rows,
        over_dp(head_rows, 1, "head_rows"),
        flops=3 * product_flops,
    )
    def over_all_experts(chunk):
        return [grads[chunk]] + [
            over_experts(grads[2 * k + chunk], k, "grads") for k in range(1, experts)
        ]

    far_chunk = over_all_experts(1)
    got_back = over_dp(core_back, 1, "token_back")
    gate_sums, beside_back = kernel_call(
        merge_body,
        [((count, 128), BF16), ((count, 2 * half + 128), BF16)],
        own_back,
        beside_back,
        got_back,
    )
    back = [own_back, got_back, over_dp(beside_back, 2, "token_back")]

    (others,) = kernel_call(
        chunk_sum_body, [((2, half - block, size), BF16)], *far_chunk, flops=1000000000
    )
    sums = over_all_experts(0) + [
        over_dp(others[:, (k - 1) * block : k * block], 4 * k, "grads") for k in range(1, quads)
    ]

    if aligned:
        (token_grad,) = kernel_call(
            lambda *refs: unpack_body(block, quads, *refs),
            [((count, features), BF16)],
            at[None],
            *back,
            scalars=1,
        )
    else:
        parts = jnp.concatenate(
            [back[0][:, :half], back[1][:count, :half], back[2][:, : 2 * half]], axis=1
        )
        token_grad = jnp.concatenate(
            [
                lax.dynamic_slice(
                    parts,
                    (0, (((at ^ b) & 3) * quads + ((at ^ b) >> 2)) * block),
                    (count, block),
                )
                for b in range(groups)
            ],
            axis=1,
        )

    (logit_grad,) = kernel_call(
        logit_body,
        [((2 * experts, count), F32)],
        gate_sums,
        back[2],
        table,
        value_routes.T,
        output_routes.T,
    )
    token_grad, logit_grad, sums = lax.optimization_barrier((token_grad, logit_grad, sums))
    value_weight_grad, output_weight_grad = kernel_call(
        lambda *refs: final_sum_body(groups, *refs), [((1, block, size), F32)] * 2, *sums
    )

    query_grad, key_grad = kernel_call(
        attention_back_body,
        [((count, size), BF16), ((count, size), BF16)],
        probs,
        queries,
        key_vectors,
        mixed_value,
        hidden_grad,
    )
    return (token_grad, query_grad, key_grad, logit_grad.T, value_weight_grad, output_weight_grad)


def solution(mesh):
    rows, banks = P(("dp", "expert"), None), P("expert", "dp", None)
    return jax.shard_map(
        on_device,
        mesh=mesh,
        in_specs=(rows,) * 6 + (banks, banks, rows),
        out_specs=(rows,) * 4 + (banks, banks),
        check_vma=False,
    )
```

```python
import math

import jax
import jax.numpy as jnp
from jax import lax
from jax.experimental import pallas as pl
from jax.experimental.pallas import tpu as pltpu
from jax.sharding import PartitionSpec as P

F32, BF16 = jnp.float32, jnp.bfloat16

def kernel_call(body, outs, *args, scalars=0, flops=0, moved=None, where=pltpu.VMEM, scratch=(), vmem=24):
    moved = moved or sum(x.size * x.dtype.itemsize for x in args) + sum(
        math.prod(s) * jnp.dtype(t).itemsize for s, t in outs
    )
    return pl.pallas_call(
        body,
        out_shape=[jax.ShapeDtypeStruct(s, t) for s, t in outs],
        in_specs=[pl.BlockSpec(memory_space=pltpu.SMEM)] * scalars
        + [pl.BlockSpec(memory_space=where)] * (len(args) - scalars),
        out_specs=[pl.BlockSpec(memory_space=pltpu.VMEM)] * len(outs),
        cost_estimate=pl.CostEstimate(flops=flops, bytes_accessed=moved, transcendentals=0),
        scratch_shapes=list(scratch),
        compiler_params=pltpu.CompilerParams(vmem_limit_bytes=vmem * 2**20),
    )(*args)


def dot(left, right):
    return jnp.dot(left, right, preferred_element_type=F32)


def dot_nt(left, right):
    return lax.dot_general(left, right, (((1,), (1,)), ((), ())), preferred_element_type=F32)


def probs_body(q_ref, k_ref, probs_ref, weights_ref):
    length = q_ref.shape[0]
    scores = dot_nt(q_ref[...], k_ref[...]) / math.sqrt(q_ref.shape[1])
    row_ids = lax.broadcasted_iota(jnp.int32, (length, length), 0)
    col_ids = lax.broadcasted_iota(jnp.int32, (length, length), 1)
    scores = jnp.where(row_ids >= col_ids, scores, -1e30)
    exponent = jnp.exp(scores - jnp.max(scores, axis=1, keepdims=True))
    probs = exponent / jnp.sum(exponent, axis=1, keepdims=True)
    probs_ref[...] = probs
    weights_ref[...] = probs.astype(BF16)


def token_table(me, logits, route_v, route_o):
    both, rows = logits.shape
    gates = jax.nn.sigmoid(logits)
    ids = lax.broadcasted_iota(jnp.int32, (both, rows), 0)
    dense = jnp.zeros((both, rows), F32)
    for routes, first in ((route_v, 0), (route_o, both // 2)):
        for j in range(2):
            route = routes[j : j + 1]
            gate = jnp.sum(jnp.where(ids == route + first, gates, 0.0), axis=0, keepdims=True)
            dense = jnp.where(ids == (route ^ me) + first, gate, dense)
    high = dense.astype(BF16).astype(F32)
    routes = [(routes ^ me).astype(F32) for routes in (route_v, route_o)]
    table = jnp.concatenate([high, dense - high] + routes, axis=0)
    return jnp.concatenate([table, jnp.zeros((128 - table.shape[0], rows), F32)], axis=0).T


def quad_table_body(experts, *refs):
    out_ref = refs[-1]
    both = 2 * experts
    for i, ref in enumerate(refs[:-1]):
        rows = ref.shape[0]
        table = ref[:, ref.shape[1] - 128 :].astype(F32)
        out_ref[i * rows : (i + 1) * rows, :] = jnp.concatenate(
            [table[:, :both] + table[:, both : 2 * both], table[:, both:]], axis=1
        )


def pack_body(block, quads, groups, bank_count, at_ref, me_ref, tokens_ref, cotangent_ref, *refs):
    bank_refs, refs = refs[:bank_count], refs[bank_count:]
    small_refs, held_refs, sems = refs[:3], refs[-4:-1], refs[-1]
    out_refs = refs[-4 - len(groups) : -4]
    small = [
        pltpu.make_async_copy(ref, held, sems.at[i])
        for i, (ref, held) in enumerate(zip(small_refs, held_refs))
    ]
    copies = [
        pltpu.make_async_copy(ref.at[0], refs[3].at[i], sems.at[3 + i])
        for i, ref in enumerate(bank_refs)
    ]
    for group, out_ref in zip(groups, out_refs):
        to = 0
        for flip in group:
            for ref in (tokens_ref, cotangent_ref):
                for k in range(quads):
                    start = pl.multiple_of((at_ref[0] ^ (4 * k + flip)) * block, block)
                    copies.append(
                        pltpu.make_async_copy(
                            ref.at[:, pl.ds(start, block)],
                            out_ref.at[:, to : to + block],
                            sems.at[3 + len(copies)],
                        )
                    )
                    to += block
    for copy in small + copies:
        copy.start()
    for copy in small:
        copy.wait()
    table = token_table(me_ref[0], *[held[...] for held in held_refs]).astype(BF16)
    for out_ref in out_refs:
        out_ref[:, out_ref.shape[1] - 128 :] = table
    for copy in copies:
        copy.wait()


def table_body(me_ref, logits_ref, vr_ref, or_ref, out_ref):
    out_ref[...] = token_table(me_ref[0], logits_ref[...], vr_ref[...], or_ref[...]).astype(BF16)


def unpack_body(block, quads, at_ref, own_ref, core_ref, beside_ref, out_ref):
    half = quads * block
    for flip, (ref, first) in enumerate(
        ((own_ref, 0), (core_ref, 0), (beside_ref, 0), (beside_ref, half))
    ):
        for k in range(quads):
            start = pl.multiple_of((at_ref[0] ^ (4 * k + flip)) * block, block)
            out_ref[:, pl.ds(start, block)] = ref[
                : out_ref.shape[0], first + k * block : first + (k + 1) * block
            ]


def turn_body(*refs):
    out_ref = refs[-1]
    for i, ref in enumerate(refs[:-1]):
        rows = ref.shape[0]
        out_ref[:, i * rows : (i + 1) * rows] = ref[:, : out_ref.shape[0]].T


def copy_body(in_ref, out_ref):
    out_ref[...] = in_ref[...]


def tail_body(in_ref, out_ref):
    out_ref[...] = in_ref[:, in_ref.shape[1] - out_ref.shape[1] :]


def turn_bank_body(size, *refs):
    for e, ref in enumerate(refs[:-1]):
        refs[-1][e * size : (e + 1) * size, :] = ref[0].T


def bank(refs, side):
    return jnp.concatenate([ref[side] for ref in refs], axis=0)


def bank_pair(refs, chunks, side, i):
    return jnp.concatenate(
        [bank(refs[e * chunks : (e + 1) * chunks], side) for e in (i, i + 1)], axis=1
    )


def expert_products(experts, chunks, half, side, row_refs, weights):
    left = jnp.concatenate([r[:, side * half : (side + 1) * half] for r in row_refs], axis=0)
    for i in range(0, experts, 2):
        product = dot(left, bank_pair(weights, chunks, side, i))
        size = product.shape[1] // 2
        yield i, product[:, :size]
        yield i + 1, product[:, size:]


def partial_body(experts, chunks, size, half, *refs):
    row_refs, table_ref, weights = refs[:4], refs[4], refs[5 : 5 + experts * chunks]
    keep_ref, send_ref = refs[-2:]
    count = row_refs[0].shape[0]
    for side in range(2):
        mixed = jnp.zeros((4 * count, size), F32)
        for e, product in expert_products(experts, chunks, half, side, row_refs, weights):
            at = side * experts + e
            mixed += table_ref[:, at : at + 1] * product
        lanes = slice(side * size, (side + 1) * size)
        keep_ref[:, lanes] = mixed[: 2 * count]
        send_ref[:, lanes] = mixed[2 * count :].astype(BF16)


def slots_body(experts, chunks, size, half, *refs):
    row_refs, table_ref, weights = refs[:4], refs[4], refs[5 : 5 + experts * chunks]
    slots_ref = refs[-1]
    count = row_refs[0].shape[0]
    for side in range(2):
        route = 4 * experts + 2 * side
        routes = [table_ref[:, route + j : route + j + 1] for j in range(2)]
        slots = [jnp.zeros((4 * count, size), F32) for _ in range(2)]
        for e, product in expert_products(experts, chunks, half, side, row_refs, weights):
            for j in range(2):
                slots[j] = jnp.where(routes[j] == float(e), product, slots[j])
        for j in range(2):
            slots_ref[:, (2 * side + j) * size : (2 * side + j + 1) * size] = slots[j].astype(BF16)


def core_sum_body(keep_ref, got_ref, sum_ref, send_ref):
    total = keep_ref[...] + got_ref[...].astype(F32)
    sum_ref[...] = total
    send_ref[...] = total.astype(BF16)


def middle_body(sum_ref, got_ref, weights_ref, far_weights_ref, mixed_ref, grad_ref, rows_ref):
    count, size = mixed_ref.shape
    for i, weights in enumerate((weights_ref[...], far_weights_ref[...])):
        total = sum_ref[i * count : (i + 1) * count, :] + got_ref[
            (1 - i) * count : (2 - i) * count, :
        ].astype(F32)
        total = total.astype(BF16)
        if i == 0:
            mixed_ref[...], grad_ref[...] = total[:, :size], total[:, size:]
        rows_ref[i * count : (i + 1) * count, :size] = dot(weights, total[:, :size]).astype(BF16)
        rows_ref[i * count : (i + 1) * count, size:] = lax.dot_general(
            weights, total[:, size:], (((0,), (0,)), ((), ())), preferred_element_type=F32
        ).astype(BF16)


def two_parts(columns):
    rows = columns[0].shape[0]
    lane = lax.broadcasted_iota(jnp.int32, (rows, 128), 1)
    block = jnp.zeros((rows, 128), F32)
    for j, column in enumerate(columns):
        high = column.astype(BF16).astype(F32)
        block = jnp.where(lane == j, high, block)
        block = jnp.where(lane == 4 + j, column - high, block)
    return block.astype(BF16)


def whole_columns(block):
    block = block.astype(F32)
    return [block[:, j : j + 1] + block[:, 4 + j : 5 + j] for j in range(4)]


def gated_rows(experts, side, table_ref, rows):
    first = side * experts
    return [
        (table_ref[:, e : e + 1] * rows).astype(BF16) for e in range(first, first + experts)
    ]


def weight_grad_body(experts, chunks, size, turned_ref, *refs):
    bank_refs, (table_ref, slots_ref), refs = refs[:2], refs[2:4], refs[4:]
    row_refs, out_refs, back_refs = refs[:2], refs[2:-3], refs[-3:]
    half, count = turned_ref.shape[0] // 2, row_refs[0].shape[0] // 2
    gate_grads = []
    for side, at in ((0, 1), (1, 0)):
        rows = jnp.concatenate([r[:, at * size : (at + 1) * size] for r in row_refs], axis=0)
        rows = rows.astype(F32)
        gated = gated_rows(experts, side, table_ref, rows)
        left = turned_ref[side * half : (side + 1) * half, :]
        for i in range(0, experts, 2):
            product = dot(left, jnp.concatenate(gated[i : i + 2], axis=1))
            for p in range(2):
                start = 0
                for out_ref in out_refs[(i + p) * chunks : (i + p + 1) * chunks]:
                    stop = start + out_ref.shape[1]
                    out_ref[side] = product[start:stop, p * size : (p + 1) * size].astype(
                        out_ref.dtype
                    )
                    start = stop
        if side == 0:
            bank_rows = jnp.concatenate([ref[...] for ref in bank_refs], axis=1)
            back = dot(jnp.concatenate(gated, axis=1), bank_rows).astype(BF16)
        for j in range(2):
            slot = slots_ref[:, (2 * side + j) * size : (2 * side + j + 1) * size].astype(F32)
            gate_grads.append(jnp.sum(rows * slot, axis=1, keepdims=True))
    gate_block = two_parts(gate_grads)
    for i, back_ref in enumerate(back_refs):
        start, stop = (i * count, (i + 1) * count) if i < 2 else (2 * count, 4 * count)
        back_ref[:, :half] = back[start:stop]
        back_ref[:, half:] = gate_block[start:stop]


def merge_body(own_ref, beside_ref, got_ref, gate_ref, send_ref):
    count, half = beside_ref.shape[0], beside_ref.shape[1] - 128
    sums = [
        two_parts(
            [
                near + far
                for near, far in zip(whole_columns(ref[:, half:]), whole_columns(got))
            ]
        )
        for ref, got in ((own_ref, got_ref[:count, half:]), (beside_ref, got_ref[count:, half:]))
    ]
    gate_ref[...] = sums[0]
    send_ref[:, :half] = beside_ref[:, :half]
    send_ref[:, half : 2 * half] = got_ref[count:, :half]
    send_ref[:, 2 * half :] = sums[1]


def logit_body(gate_ref, got_ref, table_ref, vr_ref, or_ref, out_ref):
    both, count = out_ref.shape
    got = got_ref[:, got_ref.shape[1] - 128 :]
    near, far = gate_ref[...].astype(F32).T, got.astype(F32).T
    table = table_ref[:count, :].T
    ids = lax.broadcasted_iota(jnp.int32, (both, count), 0)
    logit = jnp.zeros((both, count), F32)
    for side, route_ref in enumerate((vr_ref, or_ref)):
        first = side * (both // 2)
        for j in range(2):
            at = 2 * side + j
            grad = (near[at : at + 1] + near[4 + at : 5 + at]) + (
                far[at : at + 1] + far[4 + at : 5 + at]
            )
            here = ids.astype(F32) == table[2 * both + at : 2 * both + at + 1] + float(first)
            gate = jnp.sum(jnp.where(here, table[:both], 0.0), axis=0, keepdims=True)
            logit = jnp.where(
                ids == route_ref[j : j + 1, :] + first, grad * gate * (1.0 - gate), logit
            )
    out_ref[...] = logit


def chunk_sum_body(*refs):
    total = refs[0][...]
    for ref in refs[1:-1]:
        total += ref[...].astype(F32)
    refs[-1][...] = total.astype(BF16)


def final_sum_body(groups, *refs):
    total = refs[0][...]
    for ref in refs[1:-2]:
        total += ref[...].astype(F32)
    total = total * (1.0 / groups)
    for side in range(2):
        refs[side - 2][0] = total[side]


def attention_back_body(probs_ref, q_ref, k_ref, mixed_ref, grad_ref, query_grad_ref, key_grad_ref):
    probs = probs_ref[...]
    prob_grad = dot_nt(grad_ref[...], mixed_ref[...])
    score_grad = probs * (prob_grad - jnp.sum(prob_grad * probs, axis=1, keepdims=True))
    scaled = score_grad / math.sqrt(q_ref.shape[1])
    query_grad_ref[...] = dot(scaled.astype(BF16), k_ref[...]).astype(BF16)
    key_grad_ref[...] = dot(scaled.T.astype(BF16), q_ref[...]).astype(BF16)


def on_device(
    tokens,
    queries,
    key_vectors,
    gate_logits,
    value_routes,
    output_routes,
    value_weight,
    output_weight,
    cotangent,
):
    count, features = tokens.shape
    size = queries.shape[1]
    experts = gate_logits.shape[1] // 2
    block = value_weight.shape[1]
    groups = lax.axis_size("dp")
    quads = groups // 4
    half = quads * block
    at = lax.axis_index("dp")
    me = lax.axis_index("expert")
    aligned = block % 128 == 0

    def over_dp(x, flip, what):
        with jax.named_scope(f"{what}_dp{flip}"):
            return lax.ppermute(x, "dp", [(i, i ^ flip) for i in range(groups)])

    def over_experts(x, flip, what):
        with jax.named_scope(f"{what}_expert{flip}"):
            return lax.ppermute(x, "expert", [(i, i ^ flip) for i in range(experts)])

    def side_by_side(arrays, axis):
        return arrays[0] if len(arrays) == 1 else jnp.concatenate(arrays, axis=axis)

    routing = (gate_logits.T, value_routes.T, output_routes.T)
    flips = ((2, 3), (1,), (0,))
    if aligned:

        def pack(groups, *banks):
            return kernel_call(
                lambda *refs: pack_body(block, quads, groups, len(banks), *refs),
                [((2, block, size), BF16)] * (len(banks) // 2)
                + [((count, 2 * half * len(group) + 128), BF16) for group in groups],
                at[None],
                me[None],
                tokens,
                cotangent,
                *banks,
                *routing,
                scalars=2,
                where=pl.ANY,
                scratch=[pltpu.VMEM(x.shape, x.dtype) for x in routing]
                + [pltpu.SemaphoreType.DMA((5 + 8 * quads,))],
                vmem=60,
            )

        own_banks, sent_rows = pack(flips[:1], value_weight, output_weight)
        core_rows, own_rows = pack(flips[1:])
    else:
        own_banks = jnp.concatenate([value_weight, output_weight], axis=0)
        (own_table,) = kernel_call(
            table_body, [((count, 128), BF16)], me[None], *routing, scalars=1
        )
        sent_rows, core_rows, own_rows = [
            jnp.concatenate(
                [
                    lax.dynamic_slice(x, (0, (at ^ (4 * k + flip)) * block), (count, block))
                    for flip in group
                    for x in (tokens, cotangent)
                    for k in range(quads)
                ]
                + [own_table],
                axis=1,
            )
            for group in flips
        ]
    first_round = [over_experts(own_banks, k, "banks") for k in range(1, experts)]
    other_banks = side_by_side([over_dp(own_banks, 4 * k, "banks") for k in range(1, quads)], 1)
    beside_rows = over_dp(sent_rows, 2, "rows")
    (other_banks,) = kernel_call(
        copy_body, [(other_banks.shape, BF16)], other_banks, flops=5000000000
    )
    other_banks, core_rows = lax.optimization_barrier(
        (other_banks, core_rows)
    )
    (far_rows,) = kernel_call(
        tail_body, [((count, 2 * half + 128), BF16)], beside_rows, flops=1000000000
    )
    banks = [own_banks, other_banks]
    for k in range(1, experts):
        banks += [first_round[k - 1], over_experts(other_banks, k, "other_banks")]
    rows = [
        own_rows,
        beside_rows,
        over_dp(core_rows, 1, "rows"),
        over_dp(far_rows, 1, "far_rows"),
    ]
    probs, weights = kernel_call(
        probs_body,
        [((count, count), F32), ((count, count), BF16)],
        queries,
        key_vectors,
    )
    far_weights = over_dp(weights, 2, "weights")
    (table,) = kernel_call(
        lambda *refs: quad_table_body(experts, *refs[:4], refs[-1]),
        [((4 * count, 128), F32)],
        *rows,
        far_weights,
    )

    turned_bank = [
        kernel_call(
            lambda *refs: turn_bank_body(size, *refs),
            [((experts * size, banks[chunk].shape[1]), BF16)],
            *banks[chunk::2],
            flops=flops,
        )[0]
        for chunk, flops in enumerate((0, 4000000000))
    ]
    (turned,) = kernel_call(turn_body, [((2 * half, 4 * count), BF16)], *rows)

    product_flops = 2 * 4 * count * half * experts * size
    table, turned_bank = lax.optimization_barrier((table, turned_bank))
    keep, send = kernel_call(
        lambda *refs: partial_body(experts, 2, size, half, *refs),
        [((2 * count, 2 * size), F32), ((2 * count, 2 * size), BF16)],
        *rows,
        table,
        *banks,
        flops=2 * product_flops,
    )
    (slots,) = kernel_call(
        lambda *refs: slots_body(experts, 2, size, half, *refs),
        [((4 * count, 4 * size), BF16)],
        *rows,
        table,
        *banks,
        flops=2 * product_flops,
    )
    chip_sum, send = kernel_call(
        core_sum_body,
        [((2 * count, 2 * size), F32), ((2 * count, 2 * size), BF16)],
        keep,
        over_dp(send, 1, "partials"),
    )
    got_sum, turned, turned_bank, slots = lax.optimization_barrier(
        (over_dp(send, 2, "partials"), turned, turned_bank, slots)
    )
    mixed_value, hidden_grad, head_rows = kernel_call(
        middle_body,
        [((count, size), BF16), ((count, size), BF16), ((2 * count, 2 * size), BF16)],
        chip_sum,
        got_sum,
        weights,
        far_weights,
    )

    shapes = []
    for k in range(experts):
        kind = F32 if k == 0 else BF16
        shapes += [((2, block, size), kind), ((2, half - block, size), kind)]
    *grads, own_back, beside_back, core_back = kernel_call(
        lambda *refs: weight_grad_body(experts, 2, size, *refs),
        shapes + [((n * count, half + 128), BF16) for n in (1, 1, 2)],
        turned,
        *turned_bank,
        table,
        slots,
        head_rows,
        over_dp(head_rows, 1, "head_rows"),
        flops=3 * product_flops,
    )
    def over_all_experts(chunk):
        return [grads[chunk]] + [
            over_experts(grads[2 * k + chunk], k, "grads") for k in range(1, experts)
        ]

    far_chunk = over_all_experts(1)
    got_back = over_dp(core_back, 1, "token_back")
    gate_sums, beside_back = kernel_call(
        merge_body,
        [((count, 128), BF16), ((count, 2 * half + 128), BF16)],
        own_back,
        beside_back,
        got_back,
    )
    back = [own_back, got_back, over_dp(beside_back, 2, "token_back")]

    (others,) = kernel_call(
        chunk_sum_body, [((2, half - block, size), BF16)], *far_chunk, flops=1000000000
    )
    sums = over_all_experts(0) + [
        over_dp(others[:, (k - 1) * block : k * block], 4 * k, "grads") for k in range(1, quads)
    ]

    if aligned:
        (token_grad,) = kernel_call(
            lambda *refs: unpack_body(block, quads, *refs),
            [((count, features), BF16)],
            at[None],
            *back,
            scalars=1,
        )
    else:
        parts = jnp.concatenate(
            [back[0][:, :half], back[1][:count, :half], back[2][:, : 2 * half]], axis=1
        )
        token_grad = jnp.concatenate(
            [
                lax.dynamic_slice(
                    parts,
                    (0, (((at ^ b) & 3) * quads + ((at ^ b) >> 2)) * block),
                    (count, block),
                )
                for b in range(groups)
            ],
            axis=1,
        )

    (logit_grad,) = kernel_call(
        logit_body,
        [((2 * experts, count), F32)],
        gate_sums,
        back[2],
        table,
        value_routes.T,
        output_routes.T,
    )
    token_grad, logit_grad, sums = lax.optimization_barrier((token_grad, logit_grad, sums))
    value_weight_grad, output_weight_grad = kernel_call(
        lambda *refs: final_sum_body(groups, *refs), [((1, block, size), F32)] * 2, *sums
    )

    query_grad, key_grad = kernel_call(
        attention_back_body,
        [((count, size), BF16), ((count, size), BF16)],
        probs,
        queries,
        key_vectors,
        mixed_value,
        hidden_grad,
    )
    return (token_grad, query_grad, key_grad, logit_grad.T, value_weight_grad, output_weight_grad)


def solution(mesh):
    rows, banks = P(("dp", "expert"), None), P("expert", "dp", None)
    return jax.shard_map(
        on_device,
        mesh=mesh,
        in_specs=(rows,) * 6 + (banks, banks, rows),
        out_specs=(rows,) * 4 + (banks, banks),
        check_vma=False,
    )
```
